128 devices in a mesh: pair: 8 (over y, core), coup: 16 (over z, x).
Axes of the slice: x: 4, y: 4, z: 4, core: 2. Of those that a mesh axis runs over, the one named last changes fastest.
Arguments:
- amplitudes: bfloat16 [1024, 256, 256], P(('pair', 'coup')), may hold values from -6 to 6
- integrals: bfloat16 [1024, 256, 256], P(('pair', 'coup')), may hold values from -6 to 6
- pno_energy: float32 [1024, 256], P(('pair', 'coup')), may hold values from 0.2 to 1.5
- occ_energy: float32 [32], replicated, may hold values from -0.8 to -0.2
- occ_fock: float32 [32, 32], replicated, may hold values from -2 to 2
- row_intersection: bfloat16 [1024, 6, 256, 256], P(('pair', 'coup')), may hold values from -0.375 to 0.375
- column_intersection: bfloat16 [1024, 6, 256, 256], P(('pair', 'coup')), may hold values from -0.375 to 0.375
- row_peer: int32 [1024, 6, 1], P(('pair', 'coup')), may hold values from 0 to 15; in each aligned block of 48 rows (0 to 47, 48 to 95, ..., all dimensions but the last counted through in order) at most 4 rows name the same one
- row_offset: int32 [1024, 6], P(('pair', 'coup')), may hold values from 0 to 1
- column_partner: int32 [1024, 6], P(('pair', 'coup')), may hold values from 0 to 31
- pno_count: int32 [1024], P(('pair', 'coup')), may hold values from 128 to 256
Outputs:
- residual: bfloat16 [1024, 256, 256], P(('pair', 'coup'))
- new_amplitudes: bfloat16 [1024, 256, 256], P(('pair', 'coup'))
The draws below stay inside these ranges and needn't reach their ends.
Inputs may be any that keep to these rules, and one draw needn't show every extreme that they name: `row_peer`: among the 48 rows of one device, at most 4 name the same value, a bound that some block reaches.
All inputs are finite; a program needn't handle non-finite values.
Results may differ from the reference program's by a relative error of at most 0.009.
Values may be sent and summed in bfloat16 or wider, within the bound.
A program may use at most 128 MiB of HBM per device.

```python
import math
import jax
import jax.numpy as jnp
import numpy as np
from jax import lax

V = 256
LINKS = 6
JB = 2
IB = 4
PAIR_DEV = 8
NOCC = 32
PAIRS = 1024
CAP = 4
N_COUP = 16


def with_ends(entries, key, least, high):
    longest = entries.shape.index(max(entries.shape))
    spots = []
    for shift in (0, 1):
        where = [jax.random.randint(jax.random.fold_in(key, axis), (), 0, length) for axis, length in enumerate(entries.shape)]
        where[longest] = (where[longest] + shift) % entries.shape[longest]
        spots.append(tuple(where))
    return entries.at[spots[0]].set(least).at[spots[1]].set(high)


def steps_of(stream_key, dims, cuts, least, largest):
    loudness = 1.0
    for position, shards_of in cuts:
        heights = jax.random.uniform(jax.random.fold_in(jax.random.fold_in(stream_key, 6), position), (shards_of,), jnp.float32, least / len(cuts), largest / len(cuts))
        loudness = loudness * jnp.repeat(jnp.exp(heights), dims[position] // shards_of).reshape((-1,) + (1,) * (len(dims) - 1 - position))
    return loudness


def deal_out(stream_key, own, number, rows, amount, top, bound, skew):
    ranking = jax.random.permutation(stream_key, amount)
    packed, usual = load_shares(amount, rows * top, bound, skew, True), load_shares(amount, rows * top, bound, skew, False)
    places = jnp.arange(amount)

    def named(tallies, offset_by):
        used = int((tallies > 0).sum())
        fixed = max(1, used // 4)
        passed = fixed + (places - fixed + offset_by * (used - fixed)) % max(1, amount - fixed)
        return jnp.zeros((amount,), jnp.int32).at[ranking[jnp.where(places < fixed, places, passed)]].set(jnp.asarray(tallies, jnp.int32))

    tallies = jnp.where(number % 4 == 0, named(packed, number // 4), named(usual, number - number // 4 - 1))
    mixed = jax.random.permutation(jax.random.fold_in(own, 3), amount)
    source_of, receiver = mixed[0:amount // 2 * 2:2], mixed[1:amount // 2 * 2:2]
    room = jnp.minimum(tallies[source_of] - 1, bound - tallies[receiver]) // 2
    room = jnp.where((source_of == ranking[0]) | (receiver == ranking[0]) | (tallies[receiver] == 0), 0, jnp.maximum(room, 0))
    passed = jax.random.randint(jax.random.fold_in(own, 4), (amount // 2,), 0, 1 << 20) % (room + 1)
    tallies = tallies.at[source_of].add(-passed).at[receiver].add(passed)
    members = jnp.searchsorted(jnp.cumsum(tallies), jnp.arange(rows * top), side="right").astype(jnp.int32)
    table = members.reshape(top, rows).T
    table = table[jax.random.permutation(jax.random.fold_in(own, 1), rows)]
    offset_by = jax.random.randint(jax.random.fold_in(own, 2), (rows, 1), 0, top)
    return jnp.take_along_axis(table, (jnp.arange(top)[None, :] + offset_by) % top, axis=1)


def load_shares(count, total, reach, skew, full):
    portions = [(1 << 20) // math.isqrt(rank ** skew) + 1 for rank in range(1, count + 1)]
    largest = reach if full else min(reach, max(-(-total // count), total * portions[0] // sum(portions)))
    least = 1 if total - largest >= count - 1 else 0
    given, rest = [largest] + [least] * (count - 1), total - largest - least * (count - 1)
    while rest > 0:
        candidates = [i for i in range(1, count) if given[i] < largest] or [i for i in range(1, count) if given[i] < reach]
        whole, remaining = sum([portions[i] for i in candidates]), rest
        for i in candidates:
            extra = min(reach - given[i], max(1, remaining * portions[i] // whole), rest)
            given[i] = given[i] + extra
            rest = rest - extra
    return np.array(given)


def scatter_about(key, dims, deviation, limit, pieces=(), kind=jnp.bfloat16):
    drawn = jax.random.normal(key, dims, jnp.float32) * deviation
    if len(pieces) > 0:
        drawn = steps_of(key, dims, pieces, -0.22, 0.18) * drawn
    return jnp.clip(drawn, min=-limit, max=limit).astype(kind)


def setup_inputs(seed: int = 0) -> dict:
    key_list = jax.random.split(jax.random.key(seed), 12)
    amplitudes = scatter_about(key_list[0], (PAIRS, V, V), 1.0, 6.0, ((0, 128),))
    integrals = scatter_about(key_list[1], (PAIRS, V, V), 1.0, 6.0, ((0, 128),))
    pno_energy = jnp.clip(jnp.exp(math.log(1.5) - 2.014903 * jax.random.uniform(key_list[2], (PAIRS, V), jnp.float32) ** steps_of(key_list[2], (PAIRS, V), ((0, 128),), -0.2, 0.2)), 0.2, 1.5)
    occ_energy = jnp.clip(jax.random.uniform(key_list[3], (NOCC,), jnp.float32, -0.8, -0.2), -0.8, -0.2)
    occ_fock = scatter_about(key_list[4], (NOCC, NOCC), 0.3, 2.0, (), jnp.float32)
    row_intersection = scatter_about(key_list[5], (PAIRS, LINKS, V, V), V ** -0.5, 0.375, ((0, 128),))
    column_intersection = scatter_about(key_list[6], (PAIRS, LINKS, V, V), V ** -0.5, 0.375, ((0, 128),))
    row_peer_keys = jax.random.split(jax.random.fold_in(key_list[7], 1), PAIRS * LINKS // (PAIR_DEV * LINKS))
    row_peer_turns = jax.random.permutation(jax.random.fold_in(key_list[7], 3), PAIRS * LINKS // (PAIR_DEV * LINKS))
    row_peer = jax.vmap(lambda own, number: deal_out(jax.random.fold_in(key_list[7], 2), own, number, PAIR_DEV * LINKS, N_COUP, 1, CAP, 2))(row_peer_keys, row_peer_turns).reshape((PAIRS, LINKS, 1))
    row_offset = with_ends(jax.random.randint(key_list[8], (PAIRS, LINKS), 0, JB), jax.random.fold_in(key_list[8], 1), 0, JB - 1).astype(jnp.int32)
    column_partner = with_ends(jax.random.randint(key_list[9], (PAIRS, LINKS), 0, NOCC), jax.random.fold_in(key_list[9], 1), 0, NOCC - 1).astype(jnp.int32)
    pno_count = with_ends(jax.random.randint(key_list[10], (PAIRS,), V // 2, V + 1), jax.random.fold_in(key_list[10], 1), V // 2, V).astype(jnp.int32)
    return {"amplitudes": amplitudes, "integrals": integrals, "pno_energy": pno_energy, "occ_energy": occ_energy, "occ_fock": occ_fock, "row_intersection": row_intersection, "column_intersection": column_intersection, "row_peer": row_peer, "row_offset": row_offset, "column_partner": column_partner, "pno_count": pno_count}


def pair_index(first, second):
    return ((first // IB) * N_COUP + second // JB) * PAIR_DEV + (first % IB) * JB + second % JB


def sandwich(shared_orbitals, block_list):
    central_product = jnp.einsum("sab,sbc->sac", shared_orbitals.astype(jnp.float32), block_list.astype(jnp.float32)).astype(jnp.bfloat16)
    return jnp.einsum("sac,sdc->sad", central_product.astype(jnp.float32), shared_orbitals.astype(jnp.float32))


def reference(amplitudes, integrals, pno_energy, occ_energy, occ_fock, row_intersection, column_intersection, row_peer, row_offset, column_partner, pno_count):
    def one_pair(index):
        device = index // PAIR_DEV
        local = index % PAIR_DEV
        first = (device // N_COUP) * IB + local // JB
        second = (device % N_COUP) * JB + local % JB
        partner_k = row_peer[index, :, 0] * JB + row_offset[index]
        partner_q = column_partner[index]
        row_blocks = amplitudes[pair_index(first, partner_k)]
        column_blocks = amplitudes[pair_index(partner_q, second)]
        row_term = jnp.sum(occ_fock[partner_k, second][:, None, None] * sandwich(row_intersection[index], row_blocks), axis=0)
        column_term = jnp.sum(occ_fock[first, partner_q][:, None, None] * sandwich(column_intersection[index], column_blocks), axis=0)
        energies = pno_energy[index]
        energy_denominator = energies[:, None] + energies[None, :] - occ_energy[first] - occ_energy[second]
        present = (jnp.arange(V) < pno_count[index]).astype(jnp.float32)
        mask = present[:, None] * present[None, :]
        current = amplitudes[index].astype(jnp.float32)
        full = integrals[index].astype(jnp.float32) + energy_denominator * current - row_term - column_term
        return (mask * full).astype(jnp.bfloat16), (mask * (current - full / energy_denominator)).astype(jnp.bfloat16)

    residual, new_amplitudes = lax.map(one_pair, jnp.arange(PAIRS, dtype=jnp.int32))
    return residual, new_amplitudes
```

```python
import functools

import jax
import jax.numpy as jnp
from jax import lax
from jax.experimental import pallas as pl
from jax.experimental.pallas import tpu as pltpu
from jax.sharding import PartitionSpec as P

MESH = pl.DeviceIdType.MESH
V = 256
HALF = 128
BLOCKS = 8
LINKS = 6
TASKS = BLOCKS * LINKS
CAP = 4
SIDE = 4
N_COUP = 16

TREE = {
    (0, 1): (0, 0), (3, 0): (0, 0), (1, 1): (0, 1), (3, 3): (3, 0), (1, 2): (1, 1),
    (0, 3): (0, 0), (1, 0): (0, 0), (0, 2): (0, 1), (2, 0): (3, 0), (2, 1): (1, 1), (2, 3): (3, 3),
    (3, 1): (0, 1), (3, 2): (3, 3), (1, 3): (1, 2), (2, 2): (1, 2),
}
ROOT = (0, 0)
ORDER = [
    (0, (0, 1)), (1, (0, 1)), (0, (3, 0)), (1, (3, 0)),
    (0, (0, 3)), (0, (1, 0)), (1, (0, 3)), (1, (1, 0)),
    (0, (1, 1)), (1, (1, 1)), (0, (3, 3)), (1, (3, 3)),
    (0, (0, 2)), (0, (2, 0)), (1, (0, 2)), (1, (2, 0)),
    (0, (1, 2)), (1, (1, 2)), (0, (2, 1)), (0, (2, 3)),
    (0, (3, 1)), (1, (2, 1)),
    (0, (3, 2)), (1, (2, 3)), (1, (3, 1)), (1, (3, 2)),
    (0, (1, 3)), (0, (2, 2)), (1, (1, 3)), (1, (2, 2)),
]
INNER = [n for n in TREE if n in TREE.values()]
LEAVES = [n for n in TREE if n not in TREE.values()]
NODES = INNER + LEAVES
DIRS = [(1, 0), (3, 0), (0, 1), (0, 3)]


def sign(tree, node):
    return node if tree == 0 else ((-node[0]) % SIDE, (-node[1]) % SIDE)


def kernel(
    peer, offset, partner, count, fock, occ, amp, integ, energy, s_row, s_col,
    res_out, new_out,
    own, k_in, srow, scol, cols, slots, inner, packed, full_part, inv_den, res_v, new_v,
    lists, lists_in, lists_s, lists_in_s,
    in_sem, out_sem, list_send, list_recv, list_local, row_send, row_recv, y_send, y_recv, c_send, c_recv,
):
    pair, coup = lax.axis_index("pair"), lax.axis_index("coup")
    y, core = pair // 2, pair % 2
    z, x = coup // SIDE, coup % SIDE

    def coup_at(dz, dx):
        return lax.rem(z + dz, SIDE) * SIDE + lax.rem(x + dx, SIDE)

    def pair_at(dy, dc=0):
        return lax.rem(y + dy, SIDE) * 2 + lax.rem(core + dc, 2)

    loads = [
        pltpu.make_async_copy(amp, own, in_sem.at[0]),
        pltpu.make_async_copy(amp, cols.at[pl.ds(pair * BLOCKS, BLOCKS)], in_sem.at[1]),
        pltpu.make_async_copy(integ, k_in, in_sem.at[2]),
        pltpu.make_async_copy(s_col, scol, in_sem.at[3]),
        pltpu.make_async_copy(s_row, srow, in_sem.at[4]),
    ]
    for load in loads:
        load.start()

    barrier = pltpu.get_barrier_semaphore()
    friends = [(pair, coup_at(*d)) for d in DIRS] + [(pair_at(d), coup) for d in (1, 3)] + [(pair_at(0, 1), coup)]
    for friend in friends:
        pl.semaphore_signal(barrier, inc=1, device_id=friend, device_id_type=MESH)
    pl.semaphore_wait(barrier, len(friends))

    def rows_of(tree):
        return pl.ds(tree * HALF, HALF)

    def row_copy(tree, node):
        at, to = sign(tree, TREE[node]), sign(tree, node)
        step = ((to[0] - at[0]) % SIDE, (to[1] - at[1]) % SIDE)
        source = coup_at((-at[0]) % SIDE, (-at[1]) % SIDE)
        i = NODES.index(node)
        if node in INNER:
            src = amp.at[:, rows_of(tree), :] if at == ROOT else inner[tree * len(INNER) + INNER.index(TREE[node])]
            dst = inner[tree * len(INNER) + i]
        else:
            src = packed.at[tree * len(LEAVES) + LEAVES.index(node)]
            dst = slots.at[pl.ds(source * CAP, CAP), rows_of(tree), :]
        return pltpu.make_async_remote_copy(
            src_ref=src, dst_ref=dst, send_sem=row_send.at[tree, i], recv_sem=row_recv.at[tree, i],
            device_id=(pair, coup_at(*step)), device_id_type=MESH,
        )

    def source_at(tree, node):
        n = sign(tree, node)
        return coup_at((-n[0]) % SIDE, (-n[1]) % SIDE)

    def row_arrival(tree, node):
        i = NODES.index(node)
        if node in INNER:
            dst = inner[tree * len(INNER) + i]
        else:
            dst = slots.at[pl.ds(source_at(tree, node) * CAP, CAP), rows_of(tree), :]
        return pltpu.make_async_remote_copy(
            src_ref=dst, dst_ref=dst, send_sem=row_send.at[tree, i], recv_sem=row_recv.at[tree, i],
            device_id=(pair, coup_at(*DIRS[0])), device_id_type=MESH,
        )

    def col_region(source, part):
        return cols.at[pl.ds(source * BLOCKS + part * 4, 4)]

    def y_copy(dy, part, hop):
        source = pair if hop == 0 else pair_at((-dy) % SIDE)
        src = amp.at[pl.ds(part * 4, 4)] if hop == 0 else col_region(source, part)
        i = (0 if dy == 1 else 3) + (part if hop == 0 else 2)
        return pltpu.make_async_remote_copy(
            src_ref=src, dst_ref=col_region(source, part), send_sem=y_send.at[i], recv_sem=y_recv.at[i],
            device_id=(pair_at(dy), coup), device_id_type=MESH,
        )

    def c_copy(dy, part):
        i = dy * 2 + part
        source = pair_at(dy)
        src = amp.at[pl.ds(part * 4, 4)] if dy == 0 else col_region(source, part)
        return pltpu.make_async_remote_copy(
            src_ref=src, dst_ref=col_region(source, part), send_sem=c_send.at[i], recv_sem=c_recv.at[i],
            device_id=(pair_at(0, 1), coup), device_id_type=MESH,
        )

    started = []

    def start(copy):
        copy.start()
        started.append(copy)

    position = 0

    def send_rows(upto):
        nonlocal position
        while position < upto:
            tree, node = ORDER[position]
            parent = TREE[node]
            if parent != ROOT and (tree, parent) not in arrived:
                arrived.add((tree, parent))
                row_arrival(tree, parent).wait_recv()
            if node in LEAVES:
                pack(tree, node)
            start(row_copy(tree, node))
            position += 1

    arrived = set()

    def pack(tree, node):
        at, to = sign(tree, TREE[node]), sign(tree, node)
        step = ((to[0] - at[0]) % SIDE, (to[1] - at[1]) % SIDE)
        source = coup_at((-at[0]) % SIDE, (-at[1]) % SIDE)
        d = DIRS.index(step)
        for t in range(CAP):
            which = lists_in_s[d, 0, source * CAP + t]
            packed[tree * len(LEAVES) + LEAVES.index(node), t] = block_of(tree, TREE[node], which)

    def block_of(tree, node, which):
        if node == ROOT:
            return own[which, rows_of(tree), :]
        return inner[tree * len(INNER) + INNER.index(node)][which]

    def keep(tree, node):
        source = source_at(tree, node)
        for t in range(CAP):
            which = lists_s[0, source * CAP + t]
            slots[source * CAP + t, rows_of(tree), :] = block_of(tree, node, which)

    send_rows(4)
    start(y_copy(1, 0, 0))
    start(y_copy(3, 1, 0))
    start(y_copy(1, 1, 0))
    start(y_copy(3, 0, 0))
    start(c_copy(0, 0))
    start(c_copy(0, 1))

    lane = lax.broadcasted_iota(jnp.int32, (1, 128), 1)

    def peers_step(r, peers):
        return jnp.where(lane == r, peer[r // LINKS, r % LINKS], peers)

    peers = lax.fori_loop(0, TASKS, peers_step, jnp.full((1, 128), -1, jnp.int32))

    def list_step(r, carry):
        wanted, row_of, counts, rank = carry
        p = peer[r // LINKS, r % LINKS]
        local = (r // LINKS // 2) * 2 + offset[r // LINKS, r % LINKS]
        match = (lane // CAP) == p
        hit = match & (lane % CAP == counts)
        return (
            jnp.where(hit, local, wanted),
            jnp.where(hit, r, row_of),
            jnp.where(match, counts + 1, counts),
            rank + jnp.where((lane > r) & (peers == p), 1, 0),
        )

    zero = jnp.zeros((1, 128), jnp.int32)
    wanted, row_of, _, rank = lax.fori_loop(0, TASKS, list_step, (zero, zero, zero, zero))
    lists[0:1, :] = wanted
    lists[1:2, :] = row_of
    lists[2:3, :] = jnp.maximum(peers, 0) * CAP + rank

    def list_copy(i):
        return pltpu.make_async_remote_copy(
            src_ref=lists, dst_ref=lists_in.at[i], send_sem=list_send.at[i], recv_sem=list_recv.at[i],
            device_id=(pair, coup_at((-DIRS[i][0]) % SIDE, (-DIRS[i][1]) % SIDE)), device_id_type=MESH,
        )

    for i in range(4):
        start(list_copy(i))
    to_scalars = pltpu.make_async_copy(lists, lists_s, list_local.at[4])
    to_scalars.start()

    for load in loads[:3]:
        load.wait()

    def first_part(p, _):
        e = energy[pl.ds(p, 1), :]
        across = jnp.broadcast_to(e, (V, V))
        i, j = pair * 4 + p // 2, coup * 2 + p % 2
        den = across + across.T - occ[i] - occ[j]
        cur = own[p].astype(jnp.float32)
        full_part[p] = k_in[p].astype(jnp.float32) + den * cur
        inv_den[p] = 1.0 / den
        return 0

    lax.fori_loop(0, 4, first_part, 0)
    to_scalars.wait()
    moves = []
    for i in range(4):
        list_copy(i).wait_recv()
        moves.append(pltpu.make_async_copy(lists_in.at[i], lists_in_s.at[i], list_local.at[i]))
        moves[-1].start()
    for move in moves:
        move.wait()

    send_rows(8)
    lax.fori_loop(4, 8, first_part, 0)
    for t in range(CAP):
        slots[coup * CAP + t] = own[lists_s[0, coup * CAP + t]]

    def product(a, b, transposed=False):
        dims = (((1,), (1 if transposed else 0,)), ((), ()))
        return lax.dot_general(a, b, dims, preferred_element_type=jnp.float32)

    def row_first(source):
        def body(h, _):
            for u in range(2):
                slot = source * CAP + h * 2 + u
                r = lists_s[1, slot]
                k = source * 2 + lists_s[0, slot] % 2
                f = fock[k, coup * 2 + (r // LINKS) % 2]
                slots[slot] = (f * product(srow[r], slots[slot])).astype(jnp.bfloat16)
            return 0

        lax.fori_loop(0, CAP // 2, body, 0)

    def col_pair(p, _):
        i, parity = pair * 4 + p // 2, p % 2
        parts = []
        for s in range(LINKS):
            q = partner[p, s]
            t = cols[(q // 4) * BLOCKS + (q % 4) * 2 + parity]
            parts.append((fock[i, q] * product(scol[p * LINKS + s], t)).astype(jnp.bfloat16))
        total = jnp.zeros((V, V), jnp.float32)
        for s in range(LINKS):
            total = total + product(parts[s], scol[p * LINKS + s], True)
        full_part[p] = full_part[p] - total
        return 0

    y_copy(1, 0, 0).wait_recv()
    start(y_copy(1, 0, 1))
    start(c_copy(3, 0))
    y_copy(3, 1, 0).wait_recv()
    start(y_copy(3, 1, 1))
    start(c_copy(1, 1))
    loads[3].wait()
    loads[4].wait()
    row_first(coup)
    send_rows(12)
    for n in ((0, 1), (3, 0)):
        for tree in range(2):
            keep(tree, n)
    y_copy(1, 1, 0).wait_recv()
    start(c_copy(3, 1))
    y_copy(3, 0, 0).wait_recv()
    start(c_copy(1, 0))
    send_rows(16)
    for n in ((1, 1), (3, 3)):
        for tree in range(2):
            row_arrival(tree, n).wait_recv()
            arrived.add((tree, n))
            keep(tree, n)
    send_rows(20)
    y_copy(1, 0, 1).wait_recv()
    start(c_copy(2, 0))
    y_copy(3, 1, 1).wait_recv()
    start(c_copy(2, 1))
    leaf_done = set()

    def source_ready(*nodes):
        for n in nodes:
            for tree in range(2):
                m = sign(tree, n)
                if m in LEAVES and (tree, m) not in leaf_done:
                    leaf_done.add((tree, m))
                    row_arrival(tree, m).wait_recv()

    send_rows(22)
    for dy in range(4):
        for part in range(2):
            c_copy(dy, part).wait_recv()
    lax.fori_loop(0, 4, col_pair, 0)
    send_rows(26)
    lax.fori_loop(4, 8, col_pair, 0)
    send_rows(30)
    for tree in range(2):
        keep(tree, (1, 2))
    for n in ((0, 1), (0, 3), (1, 0), (3, 0), (0, 2), (2, 0), (1, 1), (3, 3), (2, 1), (2, 3), (1, 3), (3, 1), (1, 2), (3, 2), (2, 2)):
        source_ready(n)
        row_first(coup_at((-n[0]) % SIDE, (-n[1]) % SIDE))

    def outs(p):
        return [
            pltpu.make_async_copy(res_v.at[p], res_out.at[p], out_sem.at[0, p]),
            pltpu.make_async_copy(new_v.at[p], new_out.at[p], out_sem.at[1, p]),
        ]

    row_id = lax.broadcasted_iota(jnp.int32, (V, 1), 0)
    col_id = lax.broadcasted_iota(jnp.int32, (1, V), 1)

    def last_part(p, _):
        total = jnp.zeros((V, V), jnp.float32)
        for s in range(LINKS):
            r = p * LINKS + s
            total = total + product(slots[lists_s[2, r]], srow[r], True)
        full = full_part[p] - total
        n = count[p]
        mask = (row_id < n).astype(jnp.float32) * (col_id < n).astype(jnp.float32)
        res_v[p] = (mask * full).astype(jnp.bfloat16)
        new_v[p] = (mask * (own[p].astype(jnp.float32) - full * inv_den[p])).astype(jnp.bfloat16)
        for copy in outs(p):
            copy.start()
        return 0

    lax.fori_loop(0, BLOCKS, last_part, 0)
    for copy in started:
        copy.wait_send()
    for p in range(BLOCKS):
        for copy in outs(p):
            copy.wait()


def on_device(
    amplitudes, integrals, pno_energy, occ_energy, occ_fock, row_intersection, column_intersection,
    row_peer, row_offset, column_partner, pno_count,
):
    smem, hbm, vmem = (pl.BlockSpec(memory_space=m) for m in (pltpu.SMEM, pl.ANY, pltpu.VMEM))
    bf16, f32, i32 = jnp.bfloat16, jnp.float32, jnp.int32
    dma = pltpu.SemaphoreType.DMA
    block = (BLOCKS, V, V)
    return pl.pallas_call(
        kernel,
        out_shape=(jax.ShapeDtypeStruct(block, bf16), jax.ShapeDtypeStruct(block, bf16)),
        in_specs=[smem] * 6 + [hbm, hbm, vmem, hbm, hbm],
        out_specs=(hbm, hbm),
        scratch_shapes=[
            pltpu.VMEM(block, bf16),
            pltpu.VMEM(block, bf16),
            pltpu.VMEM((TASKS, V, V), bf16),
            pltpu.VMEM((TASKS, V, V), bf16),
            pltpu.VMEM((8 * BLOCKS, V, V), bf16),
            pltpu.VMEM((N_COUP * CAP, V, V), bf16),
            [pltpu.VMEM((BLOCKS, HALF, V), bf16)] * (2 * len(INNER)),
            pltpu.VMEM((2 * len(LEAVES), CAP, HALF, V), bf16),
            pltpu.VMEM(block, f32),
            pltpu.VMEM(block, f32),
            pltpu.VMEM(block, bf16),
            pltpu.VMEM(block, bf16),
            pltpu.VMEM((8, 128), i32),
            pltpu.VMEM((4, 8, 128), i32),
            pltpu.SMEM((8, 128), i32),
            pltpu.SMEM((4, 8, 128), i32),
            dma((5,)), dma((2, BLOCKS)), dma((4,)), dma((4,)), dma((5,)),
            dma((2, len(NODES))), dma((2, len(NODES))), dma((6,)), dma((6,)), dma((8,)), dma((8,)),
        ],
        compiler_params=pltpu.CompilerParams(
            collective_id=0, has_side_effects=True, vmem_limit_bytes=62 * 2**20
        ),
        cost_estimate=pl.CostEstimate(flops=96 * 4 * V**3, bytes_accessed=16 * 2**20, transcendentals=0),
        name="residual_iteration",
    )(
        row_peer.reshape(BLOCKS, LINKS), row_offset, column_partner, pno_count, occ_fock, occ_energy,
        amplitudes, integrals, pno_energy,
        row_intersection.reshape(TASKS, V, V), column_intersection.reshape(TASKS, V, V),
    )


def solution(mesh):
    whole = P(("pair", "coup"))
    return jax.shard_map(
        on_device,
        mesh=mesh,
        in_specs=(whole, whole, whole, P(), P(), whole, whole, whole, whole, whole, whole),
        out_specs=(whole, whole),
        check_vma=False,
    )
```

```python
import functools

import jax
import jax.numpy as jnp
from jax import lax
from jax.experimental import pallas as pl
from jax.experimental.pallas import tpu as pltpu
from jax.sharding import PartitionSpec as P

MESH = pl.DeviceIdType.MESH
V = 256
HALF = 128
BLOCKS = 8
LINKS = 6
TASKS = BLOCKS * LINKS
CAP = 4
SIDE = 4
N_COUP = 16

TREE = {
    (0, 1): (0, 0), (3, 0): (0, 0), (1, 1): (0, 1), (3, 3): (3, 0), (1, 2): (1, 1),
    (0, 3): (0, 0), (1, 0): (0, 0), (0, 2): (0, 1), (2, 0): (3, 0), (2, 1): (1, 1), (2, 3): (3, 3),
    (3, 1): (0, 1), (3, 2): (3, 3), (1, 3): (1, 2), (2, 2): (1, 2),
}
ROOT = (0, 0)
ORDER = [
    (0, (0, 1)), (1, (0, 1)), (0, (3, 0)), (1, (3, 0)),
    (0, (0, 3)), (0, (1, 0)), (1, (0, 3)), (1, (1, 0)),
    (0, (1, 1)), (1, (1, 1)), (0, (3, 3)), (1, (3, 3)),
    (0, (0, 2)), (0, (2, 0)), (1, (0, 2)), (1, (2, 0)),
    (0, (1, 2)), (1, (1, 2)), (0, (2, 1)), (0, (2, 3)),
    (0, (3, 1)), (1, (2, 1)),
    (0, (3, 2)), (1, (2, 3)), (1, (3, 1)), (1, (3, 2)),
    (0, (1, 3)), (0, (2, 2)), (1, (1, 3)), (1, (2, 2)),
]
INNER = [n for n in TREE if n in TREE.values()]
LEAVES = [n for n in TREE if n not in TREE.values()]
NODES = INNER + LEAVES
DIRS = [(1, 0), (3, 0), (0, 1), (0, 3)]


def sign(tree, node):
    return node if tree == 0 else ((-node[0]) % SIDE, (-node[1]) % SIDE)


def kernel(
    peer_h, offset_h, partner_h, count_h, fock_h, occ_h, energy_h, amp, integ, s_row, s_col,
    res_out, new_out,
    peer, offset, partner, count, fock, occ, energy,
    own, k_in, srow, scol, cols, slots, inner, packed, full_part, inv_den, res_v, new_v,
    lists, lists_in, lists_s, lists_in_s,
    small_sem, in_sem, out_sem, list_send, list_recv, list_local, row_send, row_recv, y_send, y_recv, c_send, c_recv,
):
    pair, coup = lax.axis_index("pair"), lax.axis_index("coup")
    y, core = pair // 2, pair % 2
    z, x = coup // SIDE, coup % SIDE

    def coup_at(dz, dx):
        return lax.rem(z + dz, SIDE) * SIDE + lax.rem(x + dx, SIDE)

    def pair_at(dy, dc=0):
        return lax.rem(y + dy, SIDE) * 2 + lax.rem(core + dc, 2)

    small = [
        (peer_h, peer), (offset_h, offset), (partner_h, partner), (count_h, count), (fock_h, fock), (occ_h, occ),
        (energy_h, energy),
    ]
    large = [(amp, own), (amp, cols.at[pl.ds(pair * BLOCKS, BLOCKS)]), (integ, k_in), (s_col, scol), (s_row, srow)]
    small_loads = [pltpu.make_async_copy(a, b, small_sem.at[i]) for i, (a, b) in enumerate(small)]
    loads = [pltpu.make_async_copy(a, b, in_sem.at[i]) for i, (a, b) in enumerate(large)]

    barrier = pltpu.get_barrier_semaphore()
    friends = [(pair, coup_at(*d)) for d in DIRS] + [(pair_at(d), coup) for d in (1, 3)] + [(pair_at(0, 1), coup)]
    for friend in friends:
        pl.semaphore_signal(barrier, inc=1, device_id=friend, device_id_type=MESH)
    for load in small_loads:
        load.start()
    pl.semaphore_wait(barrier, len(friends))

    def rows_of(tree):
        return pl.ds(tree * HALF, HALF)

    def row_copy(tree, node):
        at, to = sign(tree, TREE[node]), sign(tree, node)
        step = ((to[0] - at[0]) % SIDE, (to[1] - at[1]) % SIDE)
        source = coup_at((-at[0]) % SIDE, (-at[1]) % SIDE)
        i = NODES.index(node)
        if node in INNER:
            src = amp.at[:, rows_of(tree), :] if at == ROOT else inner[tree * len(INNER) + INNER.index(TREE[node])]
            dst = inner[tree * len(INNER) + i]
        else:
            src = packed.at[tree * len(LEAVES) + LEAVES.index(node)]
            dst = slots.at[pl.ds(source * CAP, CAP), rows_of(tree), :]
        return pltpu.make_async_remote_copy(
            src_ref=src, dst_ref=dst, send_sem=row_send.at[tree, i], recv_sem=row_recv.at[tree, i],
            device_id=(pair, coup_at(*step)), device_id_type=MESH,
        )

    def source_at(tree, node):
        n = sign(tree, node)
        return coup_at((-n[0]) % SIDE, (-n[1]) % SIDE)

    def row_arrival(tree, node):
        i = NODES.index(node)
        if node in INNER:
            dst = inner[tree * len(INNER) + i]
        else:
            dst = slots.at[pl.ds(source_at(tree, node) * CAP, CAP), rows_of(tree), :]
        return pltpu.make_async_remote_copy(
            src_ref=dst, dst_ref=dst, send_sem=row_send.at[tree, i], recv_sem=row_recv.at[tree, i],
            device_id=(pair, coup_at(*DIRS[0])), device_id_type=MESH,
        )

    def col_region(source, part):
        return cols.at[pl.ds(source * BLOCKS + part * 4, 4)]

    def y_copy(dy, part, hop):
        source = pair if hop == 0 else pair_at((-dy) % SIDE)
        src = amp.at[pl.ds(part * 4, 4)] if hop == 0 else col_region(source, part)
        i = (0 if dy == 1 else 3) + (part if hop == 0 else 2)
        return pltpu.make_async_remote_copy(
            src_ref=src, dst_ref=col_region(source, part), send_sem=y_send.at[i], recv_sem=y_recv.at[i],
            device_id=(pair_at(dy), coup), device_id_type=MESH,
        )

    def c_copy(dy, part):
        i = dy * 2 + part
        source = pair_at(dy)
        src = amp.at[pl.ds(part * 4, 4)] if dy == 0 else col_region(source, part)
        return pltpu.make_async_remote_copy(
            src_ref=src, dst_ref=col_region(source, part), send_sem=c_send.at[i], recv_sem=c_recv.at[i],
            device_id=(pair_at(0, 1), coup), device_id_type=MESH,
        )

    started = []

    def start(copy):
        copy.start()
        started.append(copy)

    position = 0

    def send_rows(upto):
        nonlocal position
        while position < upto:
            tree, node = ORDER[position]
            parent = TREE[node]
            if parent != ROOT and (tree, parent) not in arrived:
                arrived.add((tree, parent))
                row_arrival(tree, parent).wait_recv()
            if node in LEAVES:
                pack(tree, node)
            start(row_copy(tree, node))
            position += 1

    arrived = set()

    def pack(tree, node):
        at, to = sign(tree, TREE[node]), sign(tree, node)
        step = ((to[0] - at[0]) % SIDE, (to[1] - at[1]) % SIDE)
        source = coup_at((-at[0]) % SIDE, (-at[1]) % SIDE)
        d = DIRS.index(step)
        for t in range(CAP):
            which = lists_in_s[d, 0, source * CAP + t]
            packed[tree * len(LEAVES) + LEAVES.index(node), t] = block_of(tree, TREE[node], which)

    def block_of(tree, node, which):
        if node == ROOT:
            return own[which, rows_of(tree), :]
        return inner[tree * len(INNER) + INNER.index(node)][which]

    def keep(tree, node):
        source = source_at(tree, node)
        for t in range(CAP):
            which = lists_s[0, source * CAP + t]
            slots[source * CAP + t, rows_of(tree), :] = block_of(tree, node, which)

    send_rows(4)
    start(y_copy(1, 0, 0))
    start(y_copy(3, 1, 0))
    start(y_copy(1, 1, 0))
    start(y_copy(3, 0, 0))
    start(c_copy(0, 0))
    start(c_copy(0, 1))
    for load in loads:
        load.start()
    for load in small_loads:
        load.wait()

    lane = lax.broadcasted_iota(jnp.int32, (1, 128), 1)

    def peers_step(r, peers):
        return jnp.where(lane == r, peer[r % LINKS, 0, r // LINKS], peers)

    peers = lax.fori_loop(0, TASKS, peers_step, jnp.full((1, 128), -1, jnp.int32))

    def list_step(r, carry):
        wanted, row_of, counts, rank = carry
        p = peer[r % LINKS, 0, r // LINKS]
        local = (r // LINKS // 2) * 2 + offset[r // LINKS, r % LINKS]
        match = (lane // CAP) == p
        hit = match & (lane % CAP == counts)
        return (
            jnp.where(hit, local, wanted),
            jnp.where(hit, r, row_of),
            jnp.where(match, counts + 1, counts),
            rank + jnp.where((lane > r) & (peers == p), 1, 0),
        )

    zero = jnp.zeros((1, 128), jnp.int32)
    wanted, row_of, _, rank = lax.fori_loop(0, TASKS, list_step, (zero, zero, zero, zero))
    lists[0:1, :] = wanted
    lists[1:2, :] = row_of
    lists[2:3, :] = jnp.maximum(peers, 0) * CAP + rank

    def list_copy(i):
        return pltpu.make_async_remote_copy(
            src_ref=lists, dst_ref=lists_in.at[i], send_sem=list_send.at[i], recv_sem=list_recv.at[i],
            device_id=(pair, coup_at((-DIRS[i][0]) % SIDE, (-DIRS[i][1]) % SIDE)), device_id_type=MESH,
        )

    for i in range(4):
        start(list_copy(i))
    to_scalars = pltpu.make_async_copy(lists, lists_s, list_local.at[4])
    to_scalars.start()

    for load in loads[:3]:
        load.wait()

    def first_part(p, _):
        e = energy[pl.ds(p, 1), :]
        across = jnp.broadcast_to(e, (V, V))
        i, j = pair * 4 + p // 2, coup * 2 + p % 2
        den = across + across.T - occ[i] - occ[j]
        cur = own[p].astype(jnp.float32)
        full_part[p] = k_in[p].astype(jnp.float32) + den * cur
        inv_den[p] = 1.0 / den
        return 0

    lax.fori_loop(0, 4, first_part, 0)
    to_scalars.wait()
    moves = []
    for i in range(4):
        list_copy(i).wait_recv()
        moves.append(pltpu.make_async_copy(lists_in.at[i], lists_in_s.at[i], list_local.at[i]))
        moves[-1].start()
    for move in moves:
        move.wait()

    send_rows(8)
    lax.fori_loop(4, 8, first_part, 0)
    for t in range(CAP):
        slots[coup * CAP + t] = own[lists_s[0, coup * CAP + t]]

    def product(a, b, transposed=False):
        dims = (((1,), (1 if transposed else 0,)), ((), ()))
        return lax.dot_general(a, b, dims, preferred_element_type=jnp.float32)

    def row_first(*nodes):
        for n in nodes:
            source_ready(n)
        for n in nodes:
            source = coup_at((-n[0]) % SIDE, (-n[1]) % SIDE)
            for t in range(CAP):
                slot = source * CAP + t
                r = lists_s[1, slot]
                k = source * 2 + lists_s[0, slot] % 2
                f = fock[k, coup * 2 + (r // LINKS) % 2]
                slots[slot] = (f * product(srow[r], slots[slot])).astype(jnp.bfloat16)

    def wide(blocks):
        return jnp.concatenate(blocks, axis=1)

    def col_pair(p, _):
        i, parity = pair * 4 + p // 2, p % 2
        parts = []
        for s in range(LINKS):
            q = partner[p, s]
            t = cols[(q // 4) * BLOCKS + (q % 4) * 2 + parity]
            parts.append((fock[i, q] * product(scol[p * LINKS + s], t)).astype(jnp.bfloat16))
        intersections = [scol[p * LINKS + s] for s in range(LINKS)]
        full_part[p] = full_part[p] - product(wide(parts), wide(intersections), True)
        return 0

    leaf_done = set()

    def source_ready(n):
        for tree in range(2):
            m = sign(tree, n)
            if m in LEAVES and (tree, m) not in leaf_done:
                leaf_done.add((tree, m))
                row_arrival(tree, m).wait_recv()

    send_rows(16)
    y_copy(1, 0, 0).wait_recv()
    start(y_copy(1, 0, 1))
    start(c_copy(3, 0))
    y_copy(3, 1, 0).wait_recv()
    start(y_copy(3, 1, 1))
    start(c_copy(1, 1))
    for n in ((0, 1), (3, 0)):
        for tree in range(2):
            keep(tree, n)
    loads[4].wait()
    row_first(ROOT)
    row_first((0, 1), (0, 3))
    row_first((1, 0), (3, 0))
    y_copy(1, 1, 0).wait_recv()
    start(c_copy(3, 1))
    y_copy(3, 0, 0).wait_recv()
    start(c_copy(1, 0))
    send_rows(26)
    for n in ((1, 1), (3, 3)):
        for tree in range(2):
            keep(tree, n)
    row_first((1, 1), (3, 3))
    y_copy(1, 0, 1).wait_recv()
    start(c_copy(2, 0))
    y_copy(3, 1, 1).wait_recv()
    start(c_copy(2, 1))
    row_first((0, 2), (2, 0))
    loads[3].wait()
    for dy in range(4):
        for part in range(2):
            c_copy(dy, part).wait_recv()
    lax.fori_loop(0, 5, col_pair, 0)
    send_rows(30)
    for tree in range(2):
        keep(tree, (1, 2))
    lax.fori_loop(5, 8, col_pair, 0)
    row_first((2, 3))
    row_first((2, 1), (1, 2), (3, 2))
    row_first((3, 1), (1, 3), (2, 2))

    def outs(p):
        return [
            pltpu.make_async_copy(res_v.at[p], res_out.at[p], out_sem.at[0, p]),
            pltpu.make_async_copy(new_v.at[p], new_out.at[p], out_sem.at[1, p]),
        ]

    row_id = lax.broadcasted_iota(jnp.int32, (V, 1), 0)
    col_id = lax.broadcasted_iota(jnp.int32, (1, V), 1)

    def last_part(p, _):
        rows = [p * LINKS + s for s in range(LINKS)]
        full = full_part[p] - product(wide([slots[lists_s[2, r]] for r in rows]), wide([srow[r] for r in rows]), True)
        n = count[p]
        mask = (row_id < n).astype(jnp.float32) * (col_id < n).astype(jnp.float32)
        res_v[p] = (mask * full).astype(jnp.bfloat16)
        new_v[p] = (mask * (own[p].astype(jnp.float32) - full * inv_den[p])).astype(jnp.bfloat16)
        for copy in outs(p):
            copy.start()
        return 0

    lax.fori_loop(0, BLOCKS, last_part, 0)
    for copy in started:
        copy.wait_send()
    for p in range(BLOCKS):
        for copy in outs(p):
            copy.wait()


def copy_kernel(a, b, a_out, b_out, a_v, b_v, in_sem, out_sem):
    ways = [(a, a_v, a_out), (b, b_v, b_out)]
    steps = []
    for h in range(2):
        for w, (src, mid, dst) in enumerate(ways):
            part = pl.ds(h * BLOCKS // 2, BLOCKS // 2)
            load = pltpu.make_async_copy(src.at[part], mid.at[part], in_sem.at[w, h])
            store = pltpu.make_async_copy(mid.at[part], dst.at[part], out_sem.at[w, h])
            load.start()
            steps.append((load, store))
    for load, store in steps:
        load.wait()
        store.start()
    for _, store in steps:
        store.wait()


def on_device(
    amplitudes, integrals, pno_energy, occ_energy, occ_fock, row_intersection, column_intersection,
    row_peer, row_offset, column_partner, pno_count,
):
    hbm = pl.BlockSpec(memory_space=pl.ANY)
    bf16, f32, i32 = jnp.bfloat16, jnp.float32, jnp.int32
    dma = pltpu.SemaphoreType.DMA
    block = (BLOCKS, V, V)
    residual, new = pl.pallas_call(
        kernel,
        out_shape=(jax.ShapeDtypeStruct(block, bf16), jax.ShapeDtypeStruct(block, bf16)),
        in_specs=[hbm] * 11,
        out_specs=(hbm, hbm),
        scratch_shapes=[
            pltpu.SMEM((LINKS, 1, BLOCKS), i32), pltpu.SMEM((BLOCKS, LINKS), i32), pltpu.SMEM((BLOCKS, LINKS), i32),
            pltpu.SMEM((BLOCKS,), i32), pltpu.SMEM((32, 32), f32), pltpu.SMEM((32,), f32), pltpu.VMEM((BLOCKS, V), f32),
            pltpu.VMEM(block, bf16),
            pltpu.VMEM(block, bf16),
            pltpu.VMEM((TASKS, V, V), bf16),
            pltpu.VMEM((TASKS, V, V), bf16),
            pltpu.VMEM((8 * BLOCKS, V, V), bf16),
            pltpu.VMEM((N_COUP * CAP, V, V), bf16),
            [pltpu.VMEM((BLOCKS, HALF, V), bf16)] * (2 * len(INNER)),
            pltpu.VMEM((2 * len(LEAVES), CAP, HALF, V), bf16),
            pltpu.VMEM(block, f32),
            pltpu.VMEM(block, f32),
            pltpu.VMEM(block, bf16),
            pltpu.VMEM(block, bf16),
            pltpu.VMEM((8, 128), i32),
            pltpu.VMEM((4, 8, 128), i32),
            pltpu.SMEM((8, 128), i32),
            pltpu.SMEM((4, 8, 128), i32),
            dma((7,)), dma((5,)), dma((2, BLOCKS)), dma((4,)), dma((4,)), dma((5,)),
            dma((2, len(NODES))), dma((2, len(NODES))), dma((6,)), dma((6,)), dma((8,)), dma((8,)),
        ],
        compiler_params=pltpu.CompilerParams(
            collective_id=0, has_side_effects=True, vmem_limit_bytes=62 * 2**20
        ),
        cost_estimate=pl.CostEstimate(flops=96 * 4 * V**3, bytes_accessed=16 * 2**20, transcendentals=0),
        name="residual_iteration",
    )(
        jnp.transpose(row_peer, (1, 2, 0)), row_offset, column_partner, pno_count, occ_fock, occ_energy, pno_energy,
        amplitudes, integrals,
        row_intersection.reshape(TASKS, V, V), column_intersection.reshape(TASKS, V, V),
    )
    return pl.pallas_call(
        copy_kernel,
        out_shape=(jax.ShapeDtypeStruct(block, bf16), jax.ShapeDtypeStruct(block, bf16)),
        in_specs=[hbm, hbm],
        out_specs=(hbm, hbm),
        scratch_shapes=[pltpu.VMEM(block, bf16), pltpu.VMEM(block, bf16), dma((2, 2)), dma((2, 2))],
        compiler_params=pltpu.CompilerParams(vmem_limit_bytes=62 * 2**20),
        cost_estimate=pl.CostEstimate(flops=0, bytes_accessed=4 * 2**20, transcendentals=0),
        name="results",
    )(residual, new)


def solution(mesh):
    whole = P(("pair", "coup"))
    return jax.shard_map(
        on_device,
        mesh=mesh,
        in_specs=(whole, whole, whole, P(), P(), whole, whole, whole, whole, whole, whole),
        out_specs=(whole, whole),
        check_vma=False,
    )
```

```python
import functools

import jax
import jax.numpy as jnp
from jax import lax
from jax.experimental import pallas as pl
from jax.experimental.pallas import tpu as pltpu
from jax.sharding import PartitionSpec as P

MESH = pl.DeviceIdType.MESH
V = 256
HALF = 128
BLOCKS = 8
LINKS = 6
TASKS = BLOCKS * LINKS
CAP = 4
SIDE = 4
N_COUP = 16

TREE = {
    (0, 1): (0, 0), (3, 0): (0, 0), (1, 1): (0, 1), (3, 3): (3, 0), (1, 2): (1, 1),
    (0, 3): (0, 0), (1, 0): (0, 0), (0, 2): (0, 1), (2, 0): (3, 0), (2, 1): (1, 1), (2, 3): (3, 3),
    (3, 1): (0, 1), (3, 2): (3, 3), (1, 3): (1, 2), (2, 2): (1, 2),
}
ROOT = (0, 0)
ORDER = [
    (0, (0, 1)), (1, (0, 1)), (0, (3, 0)), (1, (3, 0)),
    (0, (0, 3)), (0, (1, 0)), (1, (0, 3)), (1, (1, 0)),
    (0, (1, 1)), (1, (1, 1)), (0, (3, 3)), (1, (3, 3)),
    (0, (0, 2)), (0, (2, 0)), (1, (0, 2)), (1, (2, 0)),
    (0, (1, 2)), (1, (1, 2)), (0, (2, 1)), (0, (2, 3)),
    (0, (3, 1)), (1, (2, 1)),
    (0, (3, 2)), (1, (2, 3)), (1, (3, 1)), (1, (3, 2)),
    (0, (1, 3)), (0, (2, 2)), (1, (1, 3)), (1, (2, 2)),
]
INNER = [n for n in TREE if n in TREE.values()]
LEAVES = [n for n in TREE if n not in TREE.values()]
NODES = INNER + LEAVES
DIRS = [(1, 0), (3, 0), (0, 1), (0, 3)]


def sign(tree, node):
    return node if tree == 0 else ((-node[0]) % SIDE, (-node[1]) % SIDE)


def kernel(
    peer_h, offset_h, partner_h, count_h, fock_h, occ_h, energy_h, amp, integ, s_row, s_col,
    res_v, new_v,
    peer, offset, partner, count, fock, occ, energy,
    own, k_in, srow, scol, cols, slots, inner, packed, full_part, inv_den,
    lists, lists_in, lists_s, lists_in_s,
    small_sem, in_sem, list_send, list_recv, list_local, row_send, row_recv, y_send, y_recv, c_send, c_recv,
):
    pair, coup = lax.axis_index("pair"), lax.axis_index("coup")
    y, core = pair // 2, pair % 2
    z, x = coup // SIDE, coup % SIDE

    def coup_at(dz, dx):
        return lax.rem(z + dz, SIDE) * SIDE + lax.rem(x + dx, SIDE)

    def pair_at(dy, dc=0):
        return lax.rem(y + dy, SIDE) * 2 + lax.rem(core + dc, 2)

    small = [
        (peer_h, peer), (offset_h, offset), (partner_h, partner), (count_h, count), (fock_h, fock), (occ_h, occ),
        (energy_h, energy),
    ]
    large = [(amp, own), (amp, cols.at[pl.ds(pair * BLOCKS, BLOCKS)]), (integ, k_in), (s_col, scol), (s_row, srow)]
    small_loads = [pltpu.make_async_copy(a, b, small_sem.at[i]) for i, (a, b) in enumerate(small)]
    loads = [pltpu.make_async_copy(a, b, in_sem.at[i]) for i, (a, b) in enumerate(large)]

    barrier = pltpu.get_barrier_semaphore()
    friends = [(pair, coup_at(*d)) for d in DIRS] + [(pair_at(d), coup) for d in (1, 3)] + [(pair_at(0, 1), coup)]
    for friend in friends:
        pl.semaphore_signal(barrier, inc=1, device_id=friend, device_id_type=MESH)
    for load in small_loads:
        load.start()
    pl.semaphore_wait(barrier, len(friends))

    def rows_of(tree):
        return pl.ds(tree * HALF, HALF)

    def row_copy(tree, node):
        at, to = sign(tree, TREE[node]), sign(tree, node)
        step = ((to[0] - at[0]) % SIDE, (to[1] - at[1]) % SIDE)
        source = coup_at((-at[0]) % SIDE, (-at[1]) % SIDE)
        i = NODES.index(node)
        if node in INNER:
            src = amp.at[:, rows_of(tree), :] if at == ROOT else inner[tree * len(INNER) + INNER.index(TREE[node])]
            dst = inner[tree * len(INNER) + i]
        else:
            src = packed.at[tree * len(LEAVES) + LEAVES.index(node)]
            dst = slots.at[pl.ds(source * CAP, CAP), rows_of(tree), :]
        return pltpu.make_async_remote_copy(
            src_ref=src, dst_ref=dst, send_sem=row_send.at[tree, i], recv_sem=row_recv.at[tree, i],
            device_id=(pair, coup_at(*step)), device_id_type=MESH,
        )

    def source_at(tree, node):
        n = sign(tree, node)
        return coup_at((-n[0]) % SIDE, (-n[1]) % SIDE)

    def row_arrival(tree, node):
        i = NODES.index(node)
        if node in INNER:
            dst = inner[tree * len(INNER) + i]
        else:
            dst = slots.at[pl.ds(source_at(tree, node) * CAP, CAP), rows_of(tree), :]
        return pltpu.make_async_remote_copy(
            src_ref=dst, dst_ref=dst, send_sem=row_send.at[tree, i], recv_sem=row_recv.at[tree, i],
            device_id=(pair, coup_at(*DIRS[0])), device_id_type=MESH,
        )

    def col_region(source, part):
        return cols.at[pl.ds(source * BLOCKS + part * 4, 4)]

    def y_copy(dy, part, hop):
        source = pair if hop == 0 else pair_at((-dy) % SIDE)
        src = amp.at[pl.ds(part * 4, 4)] if hop == 0 else col_region(source, part)
        i = (0 if dy == 1 else 3) + (part if hop == 0 else 2)
        return pltpu.make_async_remote_copy(
            src_ref=src, dst_ref=col_region(source, part), send_sem=y_send.at[i], recv_sem=y_recv.at[i],
            device_id=(pair_at(dy), coup), device_id_type=MESH,
        )

    def c_copy(dy, part):
        i = dy * 2 + part
        source = pair_at(dy)
        src = amp.at[pl.ds(part * 4, 4)] if dy == 0 else col_region(source, part)
        return pltpu.make_async_remote_copy(
            src_ref=src, dst_ref=col_region(source, part), send_sem=c_send.at[i], recv_sem=c_recv.at[i],
            device_id=(pair_at(0, 1), coup), device_id_type=MESH,
        )

    started = []

    def start(copy):
        copy.start()
        started.append(copy)

    position = 0

    def send_rows(upto):
        nonlocal position
        while position < upto:
            tree, node = ORDER[position]
            parent = TREE[node]
            if parent != ROOT and (tree, parent) not in arrived:
                arrived.add((tree, parent))
                row_arrival(tree, parent).wait_recv()
            if node in LEAVES:
                pack(tree, node)
            start(row_copy(tree, node))
            position += 1

    arrived = set()

    def pack(tree, node):
        at, to = sign(tree, TREE[node]), sign(tree, node)
        step = ((to[0] - at[0]) % SIDE, (to[1] - at[1]) % SIDE)
        source = coup_at((-at[0]) % SIDE, (-at[1]) % SIDE)
        d = DIRS.index(step)
        for t in range(CAP):
            which = lists_in_s[d, 0, source * CAP + t]
            packed[tree * len(LEAVES) + LEAVES.index(node), t] = block_of(tree, TREE[node], which)

    def block_of(tree, node, which):
        if node == ROOT:
            return own[which, rows_of(tree), :]
        return inner[tree * len(INNER) + INNER.index(node)][which]

    def keep(tree, node):
        source = source_at(tree, node)
        for t in range(CAP):
            which = lists_s[0, source * CAP + t]
            slots[source * CAP + t, rows_of(tree), :] = block_of(tree, node, which)

    send_rows(4)
    start(y_copy(1, 0, 0))
    start(y_copy(3, 1, 0))
    start(y_copy(1, 1, 0))
    start(y_copy(3, 0, 0))
    start(c_copy(0, 0))
    start(c_copy(0, 1))
    for load in loads:
        load.start()
    for load in small_loads:
        load.wait()

    lane = lax.broadcasted_iota(jnp.int32, (1, 128), 1)

    def peers_step(r, peers):
        return jnp.where(lane == r, peer[r % LINKS, 0, r // LINKS], peers)

    peers = lax.fori_loop(0, TASKS, peers_step, jnp.full((1, 128), -1, jnp.int32))

    def list_step(r, carry):
        wanted, row_of, counts, rank = carry
        p = peer[r % LINKS, 0, r // LINKS]
        local = (r // LINKS // 2) * 2 + offset[r // LINKS, r % LINKS]
        match = (lane // CAP) == p
        hit = match & (lane % CAP == counts)
        return (
            jnp.where(hit, local, wanted),
            jnp.where(hit, r, row_of),
            jnp.where(match, counts + 1, counts),
            rank + jnp.where((lane > r) & (peers == p), 1, 0),
        )

    zero = jnp.zeros((1, 128), jnp.int32)
    wanted, row_of, _, rank = lax.fori_loop(0, TASKS, list_step, (zero, zero, zero, zero))
    lists[0:1, :] = wanted
    lists[1:2, :] = row_of
    lists[2:3, :] = jnp.maximum(peers, 0) * CAP + rank

    def list_copy(i):
        return pltpu.make_async_remote_copy(
            src_ref=lists, dst_ref=lists_in.at[i], send_sem=list_send.at[i], recv_sem=list_recv.at[i],
            device_id=(pair, coup_at((-DIRS[i][0]) % SIDE, (-DIRS[i][1]) % SIDE)), device_id_type=MESH,
        )

    for i in range(4):
        start(list_copy(i))
    to_scalars = pltpu.make_async_copy(lists, lists_s, list_local.at[4])
    to_scalars.start()

    for load in loads[:3]:
        load.wait()

    def first_part(p, _):
        e = energy[pl.ds(p, 1), :]
        across = jnp.broadcast_to(e, (V, V))
        i, j = pair * 4 + p // 2, coup * 2 + p % 2
        den = across + across.T - occ[i] - occ[j]
        cur = own[p].astype(jnp.float32)
        full_part[p] = k_in[p].astype(jnp.float32) + den * cur
        inv_den[p] = 1.0 / den
        return 0

    lax.fori_loop(0, 4, first_part, 0)
    to_scalars.wait()
    moves = []
    for i in range(4):
        list_copy(i).wait_recv()
        moves.append(pltpu.make_async_copy(lists_in.at[i], lists_in_s.at[i], list_local.at[i]))
        moves[-1].start()
    for move in moves:
        move.wait()

    send_rows(8)
    lax.fori_loop(4, 8, first_part, 0)
    for t in range(CAP):
        slots[coup * CAP + t] = own[lists_s[0, coup * CAP + t]]

    def product(a, b, transposed=False):
        dims = (((1,), (1 if transposed else 0,)), ((), ()))
        return lax.dot_general(a, b, dims, preferred_element_type=jnp.float32)

    def row_first(*nodes):
        for n in nodes:
            source_ready(n)
        for n in nodes:
            source = coup_at((-n[0]) % SIDE, (-n[1]) % SIDE)
            for t in range(CAP):
                slot = source * CAP + t
                r = lists_s[1, slot]
                k = source * 2 + lists_s[0, slot] % 2
                f = fock[k, coup * 2 + (r // LINKS) % 2]
                slots[slot] = (f * product(srow[r], slots[slot])).astype(jnp.bfloat16)

    def wide(blocks):
        return jnp.concatenate(blocks, axis=1)

    def col_pair(p, _):
        i, parity = pair * 4 + p // 2, p % 2
        parts = []
        for s in range(LINKS):
            q = partner[p, s]
            t = cols[(q // 4) * BLOCKS + (q % 4) * 2 + parity]
            parts.append((fock[i, q] * product(scol[p * LINKS + s], t)).astype(jnp.bfloat16))
        intersections = [scol[p * LINKS + s] for s in range(LINKS)]
        full_part[p] = full_part[p] - product(wide(parts), wide(intersections), True)
        return 0

    leaf_done = set()

    def source_ready(n):
        for tree in range(2):
            m = sign(tree, n)
            if m in LEAVES and (tree, m) not in leaf_done:
                leaf_done.add((tree, m))
                row_arrival(tree, m).wait_recv()

    send_rows(16)
    y_copy(1, 0, 0).wait_recv()
    start(y_copy(1, 0, 1))
    start(c_copy(3, 0))
    y_copy(3, 1, 0).wait_recv()
    start(y_copy(3, 1, 1))
    start(c_copy(1, 1))
    for n in ((0, 1), (3, 0)):
        for tree in range(2):
            keep(tree, n)
    loads[4].wait()
    row_first(ROOT)
    row_first((0, 1), (0, 3))
    row_first((1, 0), (3, 0))
    y_copy(1, 1, 0).wait_recv()
    start(c_copy(3, 1))
    y_copy(3, 0, 0).wait_recv()
    start(c_copy(1, 0))
    send_rows(26)
    for n in ((1, 1), (3, 3)):
        for tree in range(2):
            keep(tree, n)
    row_first((1, 1), (3, 3))
    y_copy(1, 0, 1).wait_recv()
    start(c_copy(2, 0))
    y_copy(3, 1, 1).wait_recv()
    start(c_copy(2, 1))
    row_first((0, 2), (2, 0))
    loads[3].wait()
    for dy in range(4):
        for part in range(2):
            c_copy(dy, part).wait_recv()
    lax.fori_loop(0, 5, col_pair, 0)
    send_rows(30)
    for tree in range(2):
        keep(tree, (1, 2))
    lax.fori_loop(5, 8, col_pair, 0)
    row_first((2, 3))
    row_first((2, 1), (1, 2), (3, 2))
    row_first((3, 1), (1, 3), (2, 2))

    row_id = lax.broadcasted_iota(jnp.int32, (V, 1), 0)
    col_id = lax.broadcasted_iota(jnp.int32, (1, V), 1)

    def last_part(p):
        rows = [p * LINKS + s for s in range(LINKS)]
        full = full_part[p] - product(wide([slots[lists_s[2, r]] for r in rows]), wide([srow[r] for r in rows]), True)
        n = count[p]
        mask = (row_id < n).astype(jnp.float32) * (col_id < n).astype(jnp.float32)
        res_v[p] = (mask * full).astype(jnp.bfloat16)
        new_v[p] = (mask * (own[p].astype(jnp.float32) - full * inv_den[p])).astype(jnp.bfloat16)

    for p in range(BLOCKS):
        last_part(p)
    for copy in started:
        copy.wait_send()


def copy_kernel(a, b, a_out, b_out, sem):
    stores = [pltpu.make_async_copy(a, a_out, sem.at[0]), pltpu.make_async_copy(b, b_out, sem.at[1])]
    for store in stores:
        store.start()
    for store in stores:
        store.wait()


def on_device(
    amplitudes, integrals, pno_energy, occ_energy, occ_fock, row_intersection, column_intersection,
    row_peer, row_offset, column_partner, pno_count,
):
    hbm, vmem = pl.BlockSpec(memory_space=pl.ANY), pl.BlockSpec(memory_space=pltpu.VMEM)
    bf16, f32, i32 = jnp.bfloat16, jnp.float32, jnp.int32
    dma = pltpu.SemaphoreType.DMA
    block = (BLOCKS, V, V)
    residual, new = pl.pallas_call(
        kernel,
        out_shape=(pltpu.VMEM(block, bf16), pltpu.VMEM(block, bf16)),
        in_specs=[hbm] * 11,
        out_specs=(vmem, vmem),
        scratch_shapes=[
            pltpu.SMEM((LINKS, 1, BLOCKS), i32), pltpu.SMEM((BLOCKS, LINKS), i32), pltpu.SMEM((BLOCKS, LINKS), i32),
            pltpu.SMEM((BLOCKS,), i32), pltpu.SMEM((32, 32), f32), pltpu.SMEM((32,), f32), pltpu.VMEM((BLOCKS, V), f32),
            pltpu.VMEM(block, bf16),
            pltpu.VMEM(block, bf16),
            pltpu.VMEM((TASKS, V, V), bf16),
            pltpu.VMEM((TASKS, V, V), bf16),
            pltpu.VMEM((8 * BLOCKS, V, V), bf16),
            pltpu.VMEM((N_COUP * CAP, V, V), bf16),
            [pltpu.VMEM((BLOCKS, HALF, V), bf16)] * (2 * len(INNER)),
            pltpu.VMEM((2 * len(LEAVES), CAP, HALF, V), bf16),
            pltpu.VMEM(block, f32),
            pltpu.VMEM(block, f32),
            pltpu.VMEM((8, 128), i32),
            pltpu.VMEM((4, 8, 128), i32),
            pltpu.SMEM((8, 128), i32),
            pltpu.SMEM((4, 8, 128), i32),
            dma((7,)), dma((5,)), dma((4,)), dma((4,)), dma((5,)),
            dma((2, len(NODES))), dma((2, len(NODES))), dma((6,)), dma((6,)), dma((8,)), dma((8,)),
        ],
        compiler_params=pltpu.CompilerParams(
            collective_id=0, has_side_effects=True, vmem_limit_bytes=54 * 2**20
        ),
        cost_estimate=pl.CostEstimate(flops=96 * 4 * V**3, bytes_accessed=16 * 2**20, transcendentals=0),
        name="residual_iteration",
    )(
        jnp.transpose(row_peer, (1, 2, 0)), row_offset, column_partner, pno_count, occ_fock, occ_energy, pno_energy,
        amplitudes, integrals,
        row_intersection.reshape(TASKS, V, V), column_intersection.reshape(TASKS, V, V),
    )
    return pl.pallas_call(
        copy_kernel,
        out_shape=(jax.ShapeDtypeStruct(block, bf16), jax.ShapeDtypeStruct(block, bf16)),
        in_specs=[vmem, vmem],
        out_specs=(hbm, hbm),
        scratch_shapes=[dma((2,))],
        compiler_params=pltpu.CompilerParams(vmem_limit_bytes=54 * 2**20),
        cost_estimate=pl.CostEstimate(flops=0, bytes_accessed=4 * 2**20, transcendentals=0),
        name="results",
    )(*(pltpu.with_memory_space_constraint(a, pltpu.VMEM) for a in (residual, new)))


def solution(mesh):
    whole = P(("pair", "coup"))
    return jax.shard_map(
        on_device,
        mesh=mesh,
        in_specs=(whole, whole, whole, P(), P(), whole, whole, whole, whole, whole, whole),
        out_specs=(whole, whole),
        check_vma=False,
    )
```

```python
import functools

import jax
import jax.numpy as jnp
from jax import lax
from jax.experimental import pallas as pl
from jax.experimental.pallas import tpu as pltpu
from jax.sharding import PartitionSpec as P

MESH = pl.DeviceIdType.MESH
V = 256
HALF = 128
BLOCKS = 8
LINKS = 6
TASKS = BLOCKS * LINKS
CAP = 4
SIDE = 4
N_COUP = 16

TREE = {
    (0, 1): (0, 0), (3, 0): (0, 0), (1, 1): (0, 1), (3, 3): (3, 0), (1, 2): (1, 1),
    (0, 3): (0, 0), (1, 0): (0, 0), (0, 2): (0, 1), (2, 0): (3, 0), (2, 1): (1, 1), (2, 3): (3, 3),
    (3, 1): (0, 1), (3, 2): (3, 3), (1, 3): (1, 2), (2, 2): (1, 2),
}
ROOT = (0, 0)
ORDER = [
    (0, (0, 1), 0), (1, (0, 1), 0), (0, (3, 0), 0), (1, (3, 0), 0),
    (0, (0, 1), 1), (1, (0, 1), 1), (0, (3, 0), 1), (1, (3, 0), 1),
    (0, (1, 1), 0), (1, (1, 1), 0), (0, (3, 3), 0), (1, (3, 3), 0),
    (0, (1, 1), 1), (1, (1, 1), 1), (0, (3, 3), 1), (1, (3, 3), 1),
    (0, (1, 2), 0), (1, (1, 2), 0), (0, (1, 0), None), (1, (1, 0), None),
    (0, (1, 2), 1), (1, (1, 2), 1), (0, (2, 0), None), (1, (2, 0), None),
    (0, (2, 1), None), (1, (2, 1), None), (0, (0, 3), None), (1, (0, 3), None),
    (0, (2, 3), None), (1, (2, 3), None), (0, (3, 2), None), (1, (3, 2), None),
    (0, (3, 1), None), (1, (3, 1), None), (0, (1, 3), None), (1, (1, 3), None),
    (0, (0, 2), None), (1, (0, 2), None), (0, (2, 2), None), (1, (2, 2), None),
]
INNER = [n for n in TREE if n in TREE.values()]
LEAVES = [n for n in TREE if n not in TREE.values()]
NODES = INNER + LEAVES
DIRS = [(1, 0), (3, 0), (0, 1), (0, 3)]


def sign(tree, node):
    return node if tree == 0 else ((-node[0]) % SIDE, (-node[1]) % SIDE)


def kernel(
    peer_h, offset_h, partner_h, count_h, fock_h, occ_h, energy_h, amp, integ, s_row, s_col,
    res_v, new_v,
    peer, offset, partner, count, fock, occ, energy,
    own, k_in, srow, scol, cols, slots, inner, packed, full_part, inv_den,
    lists, lists_in, lists_s, lists_in_s,
    small_sem, in_sem, list_send, list_recv, list_local, row_send, row_recv, y_send, y_recv, c_send, c_recv,
):
    pair, coup = lax.axis_index("pair"), lax.axis_index("coup")
    y, core = pair // 2, pair % 2
    z, x = coup // SIDE, coup % SIDE

    def coup_at(dz, dx):
        return lax.rem(z + dz, SIDE) * SIDE + lax.rem(x + dx, SIDE)

    def pair_at(dy, dc=0):
        return lax.rem(y + dy, SIDE) * 2 + lax.rem(core + dc, 2)

    small = [
        (peer_h, peer), (offset_h, offset), (partner_h, partner), (count_h, count), (fock_h, fock), (occ_h, occ),
        (energy_h, energy),
    ]
    large = [(amp, own), (amp, cols.at[pl.ds(pair * BLOCKS, BLOCKS)]), (integ, k_in), (s_col, scol), (s_row, srow)]
    small_loads = [pltpu.make_async_copy(a, b, small_sem.at[i]) for i, (a, b) in enumerate(small)]
    loads = [pltpu.make_async_copy(a, b, in_sem.at[i]) for i, (a, b) in enumerate(large)]

    barrier = pltpu.get_barrier_semaphore()
    friends = [(pair, coup_at(*d)) for d in DIRS] + [(pair_at(d), coup) for d in (1, 3)] + [(pair_at(0, 1), coup)]
    for friend in friends:
        pl.semaphore_signal(barrier, inc=1, device_id=friend, device_id_type=MESH)
    for load in small_loads:
        load.start()
    pl.semaphore_wait(barrier, len(friends))

    def rows_of(tree):
        return pl.ds(tree * HALF, HALF)

    def row_copy(tree, node, part):
        at, to = sign(tree, TREE[node]), sign(tree, node)
        step = ((to[0] - at[0]) % SIDE, (to[1] - at[1]) % SIDE)
        source = coup_at((-at[0]) % SIDE, (-at[1]) % SIDE)
        if node in INNER:
            four = pl.ds(part * 4, 4)
            src = amp.at[four, rows_of(tree), :] if at == ROOT else inner_of(tree, TREE[node]).at[four]
            dst = inner_of(tree, node).at[four]
        else:
            src = packed.at[tree * len(LEAVES) + LEAVES.index(node)]
            dst = slots.at[pl.ds(source * CAP, CAP), rows_of(tree), :]
        i = NODES.index(node)
        return pltpu.make_async_remote_copy(
            src_ref=src, dst_ref=dst, send_sem=row_send.at[tree, i, part or 0], recv_sem=row_recv.at[tree, i, part or 0],
            device_id=(pair, coup_at(*step)), device_id_type=MESH,
        )

    def source_at(tree, node):
        n = sign(tree, node)
        return coup_at((-n[0]) % SIDE, (-n[1]) % SIDE)

    def inner_of(tree, node):
        return inner[tree * len(INNER) + INNER.index(node)]

    def row_arrival(tree, node, part):
        i = NODES.index(node)
        if node in INNER:
            dst = inner_of(tree, node).at[pl.ds(part * 4, 4)]
        else:
            dst = slots.at[pl.ds(source_at(tree, node) * CAP, CAP), rows_of(tree), :]
        return pltpu.make_async_remote_copy(
            src_ref=dst, dst_ref=dst, send_sem=row_send.at[tree, i, part or 0], recv_sem=row_recv.at[tree, i, part or 0],
            device_id=(pair, coup_at(*DIRS[0])), device_id_type=MESH,
        )

    def col_region(source, part):
        return cols.at[pl.ds(source * BLOCKS + part * 4, 4)]

    def y_copy(dy, part, hop):
        source = pair if hop == 0 else pair_at((-dy) % SIDE)
        src = amp.at[pl.ds(part * 4, 4)] if hop == 0 else col_region(source, part)
        i = (0 if dy == 1 else 3) + (part if hop == 0 else 2)
        return pltpu.make_async_remote_copy(
            src_ref=src, dst_ref=col_region(source, part), send_sem=y_send.at[i], recv_sem=y_recv.at[i],
            device_id=(pair_at(dy), coup), device_id_type=MESH,
        )

    def c_copy(dy, part):
        i = dy * 2 + part
        source = pair_at(dy)
        src = amp.at[pl.ds(part * 4, 4)] if dy == 0 else col_region(source, part)
        return pltpu.make_async_remote_copy(
            src_ref=src, dst_ref=col_region(source, part), send_sem=c_send.at[i], recv_sem=c_recv.at[i],
            device_id=(pair_at(0, 1), coup), device_id_type=MESH,
        )

    started = []

    def start(copy):
        copy.start()
        started.append(copy)

    position = 0
    arrived = set()

    def await_rows(tree, node, part):
        if (tree, node, part) not in arrived:
            arrived.add((tree, node, part))
            row_arrival(tree, node, part).wait_recv()

    def send_rows(upto):
        nonlocal position
        while position < upto:
            tree, node, part = ORDER[position]
            if TREE[node] != ROOT:
                for half in (0, 1) if part is None else (part,):
                    await_rows(tree, TREE[node], half)
            if node in LEAVES:
                pack(tree, node)
            start(row_copy(tree, node, part))
            position += 1

    def pack(tree, node):
        at, to = sign(tree, TREE[node]), sign(tree, node)
        step = ((to[0] - at[0]) % SIDE, (to[1] - at[1]) % SIDE)
        source = coup_at((-at[0]) % SIDE, (-at[1]) % SIDE)
        d = DIRS.index(step)
        for t in range(CAP):
            which = lists_in_s[d, 0, source * CAP + t]
            packed[tree * len(LEAVES) + LEAVES.index(node), t] = block_of(tree, TREE[node], which)

    def block_of(tree, node, which):
        if node == ROOT:
            return own[which, rows_of(tree), :]
        return inner_of(tree, node)[which]

    def keep(tree, node):
        source = source_at(tree, node)
        for half in range(2):
            await_rows(tree, node, half)
        for t in range(CAP):
            which = lists_s[0, source * CAP + t]
            slots[source * CAP + t, rows_of(tree), :] = block_of(tree, node, which)

    send_rows(8)
    start(y_copy(1, 0, 0))
    start(y_copy(3, 1, 0))
    start(y_copy(1, 1, 0))
    start(y_copy(3, 0, 0))
    start(c_copy(0, 0))
    start(c_copy(0, 1))
    for load in loads:
        load.start()
    for load in small_loads:
        load.wait()

    lane = lax.broadcasted_iota(jnp.int32, (1, 128), 1)

    def peers_step(r, peers):
        return jnp.where(lane == r, peer[r % LINKS, 0, r // LINKS], peers)

    peers = lax.fori_loop(0, TASKS, peers_step, jnp.full((1, 128), -1, jnp.int32), unroll=8)

    def list_step(r, carry):
        wanted, row_of, counts, rank = carry
        p = peer[r % LINKS, 0, r // LINKS]
        local = (r // LINKS // 2) * 2 + offset[r // LINKS, r % LINKS]
        match = (lane // CAP) == p
        hit = match & (lane % CAP == counts)
        return (
            jnp.where(hit, local, wanted),
            jnp.where(hit, r, row_of),
            jnp.where(match, counts + 1, counts),
            rank + jnp.where((lane > r) & (peers == p), 1, 0),
        )

    zero = jnp.zeros((1, 128), jnp.int32)
    wanted, row_of, _, rank = lax.fori_loop(0, TASKS, list_step, (zero, zero, zero, zero), unroll=8)
    lists[0:1, :] = wanted
    lists[1:2, :] = row_of
    lists[2:3, :] = jnp.maximum(peers, 0) * CAP + rank

    def list_copy(i):
        return pltpu.make_async_remote_copy(
            src_ref=lists, dst_ref=lists_in.at[i], send_sem=list_send.at[i], recv_sem=list_recv.at[i],
            device_id=(pair, coup_at((-DIRS[i][0]) % SIDE, (-DIRS[i][1]) % SIDE)), device_id_type=MESH,
        )

    for i in range(4):
        start(list_copy(i))
    to_scalars = pltpu.make_async_copy(lists, lists_s, list_local.at[4])
    to_scalars.start()

    send_rows(12)

    for load in loads[:3]:
        load.wait()

    def first_part(p, _):
        e = energy[pl.ds(p, 1), :]
        across = jnp.broadcast_to(e, (V, V))
        i, j = pair * 4 + p // 2, coup * 2 + p % 2
        den = across + across.T - occ[i] - occ[j]
        cur = own[p].astype(jnp.float32)
        full_part[p] = k_in[p].astype(jnp.float32) + den * cur
        inv_den[p] = 1.0 / den
        return 0

    lax.fori_loop(0, 2, first_part, 0)
    send_rows(16)
    y_copy(1, 0, 0).wait_recv()
    start(y_copy(1, 0, 1))
    start(c_copy(3, 0))
    y_copy(3, 1, 0).wait_recv()
    start(y_copy(3, 1, 1))
    start(c_copy(1, 1))
    to_scalars.wait()
    moves = []
    for i in range(4):
        list_copy(i).wait_recv()
        moves.append(pltpu.make_async_copy(lists_in.at[i], lists_in_s.at[i], list_local.at[i]))
        moves[-1].start()
    for move in moves:
        move.wait()

    lax.fori_loop(2, 8, first_part, 0)
    for t in range(CAP):
        slots[coup * CAP + t] = own[lists_s[0, coup * CAP + t]]

    def product(a, b, transposed=False):
        dims = (((1,), (1 if transposed else 0,)), ((), ()))
        return lax.dot_general(a, b, dims, preferred_element_type=jnp.float32)

    def row_first(*nodes):
        for n in nodes:
            source_ready(n)
        for n in nodes:
            source = coup_at((-n[0]) % SIDE, (-n[1]) % SIDE)
            for t in range(CAP):
                slot = source * CAP + t
                r = lists_s[1, slot]
                k = source * 2 + lists_s[0, slot] % 2
                f = fock[k, coup * 2 + (r // LINKS) % 2]
                slots[slot] = (f * product(srow[r], slots[slot])).astype(jnp.bfloat16)

    def wide(blocks):
        return jnp.concatenate(blocks, axis=1)

    def col_pair(p, _):
        i, parity = pair * 4 + p // 2, p % 2
        parts = []
        for s in range(LINKS):
            q = partner[p, s]
            t = cols[(q // 4) * BLOCKS + (q % 4) * 2 + parity]
            parts.append((fock[i, q] * product(scol[p * LINKS + s], t)).astype(jnp.bfloat16))
        intersections = [scol[p * LINKS + s] for s in range(LINKS)]
        full_part[p] = full_part[p] - product(wide(parts), wide(intersections), True)
        return 0

    leaf_done = set()

    def source_ready(n):
        for tree in range(2):
            m = sign(tree, n)
            if m in LEAVES and (tree, m) not in leaf_done:
                leaf_done.add((tree, m))
                row_arrival(tree, m, None).wait_recv()

    for n in ((0, 1), (3, 0)):
        for tree in range(2):
            keep(tree, n)
    send_rows(20)
    loads[4].wait()
    row_first(ROOT)
    y_copy(1, 1, 0).wait_recv()
    start(c_copy(3, 1))
    y_copy(3, 0, 0).wait_recv()
    start(c_copy(1, 0))
    send_rows(34)
    for n in ((1, 1), (3, 3)):
        for tree in range(2):
            keep(tree, n)
    row_first((1, 1), (3, 3))
    row_first((1, 0), (3, 0))
    loads[3].wait()
    send_rows(40)
    y_copy(1, 0, 1).wait_recv()
    start(c_copy(2, 0))
    y_copy(3, 1, 1).wait_recv()
    start(c_copy(2, 1))
    for tree in range(2):
        keep(tree, (1, 2))
    row_first((2, 0))
    for dy in range(4):
        for part in range(2):
            c_copy(dy, part).wait_recv()
    lax.fori_loop(0, 3, col_pair, 0)
    row_first((0, 1), (0, 3))
    lax.fori_loop(3, 8, col_pair, 0)
    row_first((2, 1), (2, 3), (1, 2), (3, 2))
    row_first((1, 3), (3, 1))
    row_first((0, 2), (2, 2))

    row_id = lax.broadcasted_iota(jnp.int32, (V, 1), 0)
    col_id = lax.broadcasted_iota(jnp.int32, (1, V), 1)

    def last_part(p):
        rows = [p * LINKS + s for s in range(LINKS)]
        full = full_part[p] - product(wide([slots[lists_s[2, r]] for r in rows]), wide([srow[r] for r in rows]), True)
        n = count[p]
        mask = (row_id < n).astype(jnp.float32) * (col_id < n).astype(jnp.float32)
        res_v[p] = (mask * full).astype(jnp.bfloat16)
        new_v[p] = (mask * (own[p].astype(jnp.float32) - full * inv_den[p])).astype(jnp.bfloat16)

    for p in range(BLOCKS):
        last_part(p)
    for copy in started:
        copy.wait_send()


def copy_kernel(a, b, a_out, b_out, sem):
    stores = [pltpu.make_async_copy(a, a_out, sem.at[0]), pltpu.make_async_copy(b, b_out, sem.at[1])]
    for store in stores:
        store.start()
    for store in stores:
        store.wait()


def on_device(
    amplitudes, integrals, pno_energy, occ_energy, occ_fock, row_intersection, column_intersection,
    row_peer, row_offset, column_partner, pno_count,
):
    hbm, vmem = pl.BlockSpec(memory_space=pl.ANY), pl.BlockSpec(memory_space=pltpu.VMEM)
    bf16, f32, i32 = jnp.bfloat16, jnp.float32, jnp.int32
    dma = pltpu.SemaphoreType.DMA
    block = (BLOCKS, V, V)
    residual, new = pl.pallas_call(
        kernel,
        out_shape=(pltpu.VMEM(block, bf16), pltpu.VMEM(block, bf16)),
        in_specs=[hbm] * 11,
        out_specs=(vmem, vmem),
        scratch_shapes=[
            pltpu.SMEM((LINKS, 1, BLOCKS), i32), pltpu.SMEM((BLOCKS, LINKS), i32), pltpu.SMEM((BLOCKS, LINKS), i32),
            pltpu.SMEM((BLOCKS,), i32), pltpu.SMEM((32, 32), f32), pltpu.SMEM((32,), f32), pltpu.VMEM((BLOCKS, V), f32),
            pltpu.VMEM(block, bf16),
            pltpu.VMEM(block, bf16),
            pltpu.VMEM((TASKS, V, V), bf16),
            pltpu.VMEM((TASKS, V, V), bf16),
            pltpu.VMEM((8 * BLOCKS, V, V), bf16),
            pltpu.VMEM((N_COUP * CAP, V, V), bf16),
            [pltpu.VMEM((BLOCKS, HALF, V), bf16)] * (2 * len(INNER)),
            pltpu.VMEM((2 * len(LEAVES), CAP, HALF, V), bf16),
            pltpu.VMEM(block, f32),
            pltpu.VMEM(block, f32),
            pltpu.VMEM((8, 128), i32),
            pltpu.VMEM((4, 8, 128), i32),
            pltpu.SMEM((8, 128), i32),
            pltpu.SMEM((4, 8, 128), i32),
            dma((7,)), dma((5,)), dma((4,)), dma((4,)), dma((5,)),
            dma((2, len(NODES), 2)), dma((2, len(NODES), 2)), dma((6,)), dma((6,)), dma((8,)), dma((8,)),
        ],
        compiler_params=pltpu.CompilerParams(
            collective_id=0, has_side_effects=True, vmem_limit_bytes=54 * 2**20
        ),
        cost_estimate=pl.CostEstimate(flops=96 * 4 * V**3, bytes_accessed=16 * 2**20, transcendentals=0),
        name="residual_iteration",
    )(
        jnp.transpose(row_peer, (1, 2, 0)), row_offset, column_partner, pno_count, occ_fock, occ_energy, pno_energy,
        amplitudes, integrals,
        row_intersection.reshape(TASKS, V, V), column_intersection.reshape(TASKS, V, V),
    )
    return pl.pallas_call(
        copy_kernel,
        out_shape=(jax.ShapeDtypeStruct(block, bf16), jax.ShapeDtypeStruct(block, bf16)),
        in_specs=[vmem, vmem],
        out_specs=(hbm, hbm),
        scratch_shapes=[dma((2,))],
        compiler_params=pltpu.CompilerParams(vmem_limit_bytes=54 * 2**20),
        cost_estimate=pl.CostEstimate(flops=0, bytes_accessed=4 * 2**20, transcendentals=0),
        name="results",
    )(*(pltpu.with_memory_space_constraint(a, pltpu.VMEM) for a in (residual, new)))


def solution(mesh):
    whole = P(("pair", "coup"))
    return jax.shard_map(
        on_device,
        mesh=mesh,
        in_specs=(whole, whole, whole, P(), P(), whole, whole, whole, whole, whole, whole),
        out_specs=(whole, whole),
        check_vma=False,
    )
```

```python
import functools

import jax
import jax.numpy as jnp
from jax import lax
from jax.experimental import pallas as pl
from jax.experimental.pallas import tpu as pltpu
from jax.sharding import PartitionSpec as P

MESH = pl.DeviceIdType.MESH
V = 256
HALF = 128
BLOCKS = 8
LINKS = 6
TASKS = BLOCKS * LINKS
CAP = 4
SIDE = 4
N_COUP = 16

TREE = {
    (0, 1): (0, 0), (3, 0): (0, 0), (1, 1): (0, 1), (3, 3): (3, 0), (1, 2): (1, 1),
    (0, 3): (0, 0), (1, 0): (0, 0), (0, 2): (0, 1), (2, 0): (3, 0), (2, 1): (1, 1), (2, 3): (3, 3),
    (3, 1): (0, 1), (3, 2): (3, 3), (1, 3): (1, 2), (2, 2): (1, 2),
}
ROOT = (0, 0)
ORDER = [
    (0, (0, 1), 0), (1, (0, 1), 0), (0, (3, 0), 0), (1, (3, 0), 0),
    (0, (0, 1), 1), (1, (0, 1), 1), (0, (3, 0), 1), (1, (3, 0), 1),
    (0, (1, 1), 0), (1, (1, 1), 0), (0, (3, 3), 0), (1, (3, 3), 0),
    (0, (1, 1), 1), (1, (1, 1), 1), (0, (3, 3), 1), (1, (3, 3), 1),
    (0, (1, 2), 0), (1, (1, 2), 0), (0, (1, 0), None), (1, (1, 0), None),
    (0, (1, 2), 1), (1, (1, 2), 1), (0, (2, 0), None), (1, (2, 0), None),
    (0, (2, 1), None), (1, (2, 1), None), (0, (0, 3), None), (1, (0, 3), None),
    (0, (2, 3), None), (1, (2, 3), None), (0, (3, 2), None), (1, (3, 2), None),
    (0, (3, 1), None), (1, (3, 1), None), (0, (1, 3), None), (1, (1, 3), None),
    (0, (0, 2), 0), (1, (0, 2), 0), (0, (2, 2), 0), (1, (2, 2), 0),
    (0, (0, 2), 1), (1, (0, 2), 1), (0, (2, 2), 1), (1, (2, 2), 1),
]
LAST = [(0, 2), (2, 2)]
INNER = [n for n in TREE if n in TREE.values()]
LEAVES = [n for n in TREE if n not in TREE.values()]
NODES = INNER + LEAVES
DIRS = [(1, 0), (3, 0), (0, 1), (0, 3)]


def sign(tree, node):
    return node if tree == 0 else ((-node[0]) % SIDE, (-node[1]) % SIDE)


def kernel(
    peer_h, offset_h, partner_h, count_h, fock_h, occ_h, energy_h, amp, integ, s_row, s_col,
    own, full_part, inv_den, late_part, late_pair,
    peer, offset, partner, count, fock, occ, energy,
    k_in, srow, scol, cols, slots, late, inner, packed,
    lists, lists_in, lists_s, lists_in_s,
    small_sem, in_sem, list_send, list_recv, list_local, row_send, row_recv, y_send, y_recv, c_send, c_recv,
):
    pair, coup = lax.axis_index("pair"), lax.axis_index("coup")
    y, core = pair // 2, pair % 2
    z, x = coup // SIDE, coup % SIDE

    def coup_at(dz, dx):
        return lax.rem(z + dz, SIDE) * SIDE + lax.rem(x + dx, SIDE)

    def pair_at(dy, dc=0):
        return lax.rem(y + dy, SIDE) * 2 + lax.rem(core + dc, 2)

    small = [
        (peer_h, peer), (offset_h, offset), (partner_h, partner), (count_h, count), (fock_h, fock), (occ_h, occ),
        (energy_h, energy),
    ]
    large = [(amp, own), (amp, cols.at[pl.ds(pair * BLOCKS, BLOCKS)]), (integ, k_in), (s_col, scol), (s_row, srow)]
    small_loads = [pltpu.make_async_copy(a, b, small_sem.at[i]) for i, (a, b) in enumerate(small)]
    loads = [pltpu.make_async_copy(a, b, in_sem.at[i]) for i, (a, b) in enumerate(large)]

    barrier = pltpu.get_barrier_semaphore()
    friends = [(pair, coup_at(*d)) for d in DIRS] + [(pair_at(d), coup) for d in (1, 3)] + [(pair_at(0, 1), coup)]
    for friend in friends:
        pl.semaphore_signal(barrier, inc=1, device_id=friend, device_id_type=MESH)
    for load in small_loads:
        load.start()
    pl.semaphore_wait(barrier, len(friends))

    def rows_of(tree):
        return pl.ds(tree * HALF, HALF)

    def leaf_place(source, tree, node, part):
        if part is None:
            return slots.at[pl.ds(source * CAP, CAP), rows_of(tree), :]
        if part == 0:
            return slots.at[pl.ds(source * CAP, 2), rows_of(tree), :]
        return late.at[pl.ds(LAST.index(node) * 2, 2), rows_of(tree), :]

    def row_copy(tree, node, part):
        at, to = sign(tree, TREE[node]), sign(tree, node)
        step = ((to[0] - at[0]) % SIDE, (to[1] - at[1]) % SIDE)
        source = coup_at((-at[0]) % SIDE, (-at[1]) % SIDE)
        if node in INNER:
            four = pl.ds(part * 4, 4)
            src = amp.at[four, rows_of(tree), :] if at == ROOT else inner_of(tree, TREE[node]).at[four]
            dst = inner_of(tree, node).at[four]
        else:
            src = packed.at[tree * len(LEAVES) + LEAVES.index(node)]
            if part is not None:
                src = src.at[pl.ds(part * 2, 2)]
            dst = leaf_place(source, tree, node, part)
        i = NODES.index(node)
        return pltpu.make_async_remote_copy(
            src_ref=src, dst_ref=dst, send_sem=row_send.at[tree, i, part or 0], recv_sem=row_recv.at[tree, i, part or 0],
            device_id=(pair, coup_at(*step)), device_id_type=MESH,
        )

    def source_at(tree, node):
        n = sign(tree, node)
        return coup_at((-n[0]) % SIDE, (-n[1]) % SIDE)

    def inner_of(tree, node):
        return inner[tree * len(INNER) + INNER.index(node)]

    def row_arrival(tree, node, part):
        i = NODES.index(node)
        if node in INNER:
            dst = inner_of(tree, node).at[pl.ds(part * 4, 4)]
        else:
            dst = leaf_place(source_at(tree, node), tree, node, part)
        return pltpu.make_async_remote_copy(
            src_ref=dst, dst_ref=dst, send_sem=row_send.at[tree, i, part or 0], recv_sem=row_recv.at[tree, i, part or 0],
            device_id=(pair, coup_at(*DIRS[0])), device_id_type=MESH,
        )

    def col_region(source, part):
        return cols.at[pl.ds(source * BLOCKS + part * 4, 4)]

    def y_copy(dy, part, hop):
        source = pair if hop == 0 else pair_at((-dy) % SIDE)
        src = amp.at[pl.ds(part * 4, 4)] if hop == 0 else col_region(source, part)
        i = (0 if dy == 1 else 3) + (part if hop == 0 else 2)
        return pltpu.make_async_remote_copy(
            src_ref=src, dst_ref=col_region(source, part), send_sem=y_send.at[i], recv_sem=y_recv.at[i],
            device_id=(pair_at(dy), coup), device_id_type=MESH,
        )

    def c_copy(dy, part):
        i = dy * 2 + part
        source = pair_at(dy)
        src = amp.at[pl.ds(part * 4, 4)] if dy == 0 else col_region(source, part)
        return pltpu.make_async_remote_copy(
            src_ref=src, dst_ref=col_region(source, part), send_sem=c_send.at[i], recv_sem=c_recv.at[i],
            device_id=(pair_at(0, 1), coup), device_id_type=MESH,
        )

    started = []

    def start(copy):
        copy.start()
        started.append(copy)

    position = 0
    arrived = set()

    def await_rows(tree, node, part):
        if (tree, node, part) not in arrived:
            arrived.add((tree, node, part))
            row_arrival(tree, node, part).wait_recv()

    def send_rows(upto):
        nonlocal position
        while position < upto:
            tree, node, part = ORDER[position]
            if TREE[node] != ROOT:
                for half in (0, 1) if node in LEAVES else (part,):
                    await_rows(tree, TREE[node], half)
            if node in LEAVES and part != 1:
                pack(tree, node)
            start(row_copy(tree, node, part))
            position += 1

    def pack(tree, node):
        at, to = sign(tree, TREE[node]), sign(tree, node)
        step = ((to[0] - at[0]) % SIDE, (to[1] - at[1]) % SIDE)
        source = coup_at((-at[0]) % SIDE, (-at[1]) % SIDE)
        d = DIRS.index(step)
        for t in range(CAP):
            which = lists_in_s[d, 0, source * CAP + t]
            packed[tree * len(LEAVES) + LEAVES.index(node), t] = block_of(tree, TREE[node], which)

    def block_of(tree, node, which):
        if node == ROOT:
            return own[which, rows_of(tree), :]
        return inner_of(tree, node)[which]

    def keep(tree, node):
        source = source_at(tree, node)
        for half in range(2):
            await_rows(tree, node, half)
        for t in range(CAP):
            which = lists_s[0, source * CAP + t]
            slots[source * CAP + t, rows_of(tree), :] = block_of(tree, node, which)

    send_rows(8)
    start(y_copy(1, 0, 0))
    start(y_copy(3, 1, 0))
    start(y_copy(1, 1, 0))
    start(y_copy(3, 0, 0))
    start(c_copy(0, 0))
    start(c_copy(0, 1))
    for load in loads:
        load.start()
    for load in small_loads:
        load.wait()

    lane = lax.broadcasted_iota(jnp.int32, (1, 128), 1)

    def peers_step(r, peers):
        return jnp.where(lane == r, peer[r % LINKS, 0, r // LINKS], peers)

    peers = lax.fori_loop(0, TASKS, peers_step, jnp.full((1, 128), -1, jnp.int32), unroll=8)

    def list_step(r, carry):
        wanted, row_of, counts, rank = carry
        p = peer[r % LINKS, 0, r // LINKS]
        local = (r // LINKS // 2) * 2 + offset[r // LINKS, r % LINKS]
        match = (lane // CAP) == p
        hit = match & (lane % CAP == counts)
        return (
            jnp.where(hit, local, wanted),
            jnp.where(hit, r, row_of),
            jnp.where(match, counts + 1, counts),
            rank + jnp.where((lane > r) & (peers == p), 1, 0),
        )

    zero = jnp.zeros((1, 128), jnp.int32)
    wanted, row_of, _, rank = lax.fori_loop(0, TASKS, list_step, (zero, zero - 1, zero, zero), unroll=8)
    lists[0:1, :] = wanted
    lists[1:2, :] = row_of
    lists[2:3, :] = jnp.maximum(peers, 0) * CAP + rank

    def list_copy(i):
        return pltpu.make_async_remote_copy(
            src_ref=lists, dst_ref=lists_in.at[i], send_sem=list_send.at[i], recv_sem=list_recv.at[i],
            device_id=(pair, coup_at((-DIRS[i][0]) % SIDE, (-DIRS[i][1]) % SIDE)), device_id_type=MESH,
        )

    for i in range(4):
        start(list_copy(i))
    to_scalars = pltpu.make_async_copy(lists, lists_s, list_local.at[4])
    to_scalars.start()

    send_rows(12)

    for load in loads[:3]:
        load.wait()

    def first_part(p, _):
        e = energy[pl.ds(p, 1), :]
        across = jnp.broadcast_to(e, (V, V))
        i, j = pair * 4 + p // 2, coup * 2 + p % 2
        den = across + across.T - occ[i] - occ[j]
        cur = own[p].astype(jnp.float32)
        full_part[p] = k_in[p].astype(jnp.float32) + den * cur
        inv_den[p] = 1.0 / den
        return 0

    lax.fori_loop(0, 2, first_part, 0)
    send_rows(16)
    y_copy(1, 0, 0).wait_recv()
    start(y_copy(1, 0, 1))
    start(c_copy(3, 0))
    y_copy(3, 1, 0).wait_recv()
    start(y_copy(3, 1, 1))
    start(c_copy(1, 1))
    to_scalars.wait()
    moves = []
    for i in range(4):
        list_copy(i).wait_recv()
        moves.append(pltpu.make_async_copy(lists_in.at[i], lists_in_s.at[i], list_local.at[i]))
        moves[-1].start()
    for move in moves:
        move.wait()

    lax.fori_loop(2, 8, first_part, 0)
    for n in LAST:
        for t in (2, 3):
            slots[coup_at((-n[0]) % SIDE, (-n[1]) % SIDE) * CAP + t] = jnp.zeros((V, V), jnp.bfloat16)
    for t in range(CAP):
        slots[coup * CAP + t] = own[lists_s[0, coup * CAP + t]]

    def product(a, b, transposed=False):
        dims = (((1,), (1 if transposed else 0,)), ((), ()))
        return lax.dot_general(a, b, dims, preferred_element_type=jnp.float32)

    def link_of(slot, source):
        r = lists_s[1, slot]
        some = jnp.maximum(r, 0)
        f = fock[source * 2 + lists_s[0, slot] % 2, coup * 2 + (some // LINKS) % 2]
        return some, jnp.where(r < 0, 0.0, f)

    def row_first(*nodes):
        for n in nodes:
            source_ready(n)
        for n in nodes:
            source = coup_at((-n[0]) % SIDE, (-n[1]) % SIDE)
            for t in range(2 if n in LAST else CAP):
                slot = source * CAP + t
                r, f = link_of(slot, source)
                slots[slot] = (f * product(srow[r], slots[slot])).astype(jnp.bfloat16)

    def wide(blocks):
        return jnp.concatenate(blocks, axis=1)

    def col_pair(p, _):
        i, parity = pair * 4 + p // 2, p % 2
        parts = []
        for s in range(LINKS):
            q = partner[p, s]
            t = cols[(q // 4) * BLOCKS + (q % 4) * 2 + parity]
            parts.append((fock[i, q] * product(scol[p * LINKS + s], t)).astype(jnp.bfloat16))
        intersections = [scol[p * LINKS + s] for s in range(LINKS)]
        full_part[p] = full_part[p] - product(wide(parts), wide(intersections), True)
        return 0

    leaf_done = set()

    def source_ready(n):
        for tree in range(2):
            m = sign(tree, n)
            if m in LEAVES and (tree, m) not in leaf_done:
                leaf_done.add((tree, m))
                row_arrival(tree, m, 0 if m in LAST else None).wait_recv()

    for n in ((0, 1), (3, 0)):
        for tree in range(2):
            keep(tree, n)
    send_rows(20)
    loads[4].wait()
    row_first(ROOT)
    y_copy(1, 1, 0).wait_recv()
    start(c_copy(3, 1))
    y_copy(3, 0, 0).wait_recv()
    start(c_copy(1, 0))
    send_rows(34)
    for n in ((1, 1), (3, 3)):
        for tree in range(2):
            keep(tree, n)
    row_first((1, 1), (3, 3))
    row_first((1, 0), (3, 0))
    loads[3].wait()
    send_rows(44)
    y_copy(1, 0, 1).wait_recv()
    start(c_copy(2, 0))
    y_copy(3, 1, 1).wait_recv()
    start(c_copy(2, 1))
    for tree in range(2):
        keep(tree, (1, 2))
    row_first((2, 0))
    for dy in range(4):
        for part in range(2):
            c_copy(dy, part).wait_recv()
    lax.fori_loop(0, 3, col_pair, 0)
    row_first((0, 1), (0, 3))
    lax.fori_loop(3, 8, col_pair, 0)
    row_first((2, 1), (2, 3), (1, 2), (3, 2))
    row_first((1, 3), (3, 1))
    row_first((0, 2), (2, 2))

    row_id = lax.broadcasted_iota(jnp.int32, (V, 1), 0)
    col_id = lax.broadcasted_iota(jnp.int32, (1, V), 1)

    def mask_of(p):
        return (row_id < count[p]).astype(jnp.float32) * (col_id < count[p]).astype(jnp.float32)

    for p in range(BLOCKS):
        rows = [p * LINKS + s for s in range(LINKS)]
        mask = mask_of(p)
        term = product(wide([slots[lists_s[2, r]] for r in rows]), wide([srow[r] for r in rows]), True)
        full_part[p] = mask * (full_part[p] - term)
        own[p] = (mask * own[p].astype(jnp.float32)).astype(jnp.bfloat16)

    for tree in range(2):
        for n in LAST:
            await_rows(tree, n, 1)
    middles = []
    for u in range(2 * len(LAST)):
        n = LAST[u // 2]
        source = coup_at((-n[0]) % SIDE, (-n[1]) % SIDE)
        r, f = link_of(source * CAP + 2 + u % 2, source)
        middles.append((r, (f * product(srow[r], late[u])).astype(jnp.bfloat16)))
    for u, (r, middle) in enumerate(middles):
        p = r // LINKS
        late_part[u] = mask_of(p) * product(middle, srow[r], True)
        late_pair[u : u + 1, :] = jnp.full((1, 128), p, jnp.int32)

    for copy in started:
        copy.wait_send()


def results_kernel(own, _, inv_den, late_part, late_pair, res_out, new_out, full_part, res_v, new_v, sem):
    stores = []
    pairs = [jnp.max(late_pair[u : u + 1, :]) for u in range(2 * len(LAST))]
    for u, p in enumerate(pairs):
        full_part[p] = full_part[p] - late_part[u]
    for p in range(BLOCKS):
        full = full_part[p]
        res_v[p] = full.astype(jnp.bfloat16)
        new_v[p] = (own[p].astype(jnp.float32) - full * inv_den[p]).astype(jnp.bfloat16)
        stores.append(pltpu.make_async_copy(res_v.at[p], res_out.at[p], sem.at[0, p]))
        stores.append(pltpu.make_async_copy(new_v.at[p], new_out.at[p], sem.at[1, p]))
        stores[-2].start()
        stores[-1].start()
    for store in stores:
        store.wait()


def on_device(
    amplitudes, integrals, pno_energy, occ_energy, occ_fock, row_intersection, column_intersection,
    row_peer, row_offset, column_partner, pno_count,
):
    hbm, vmem = pl.BlockSpec(memory_space=pl.ANY), pl.BlockSpec(memory_space=pltpu.VMEM)
    bf16, f32, i32 = jnp.bfloat16, jnp.float32, jnp.int32
    dma = pltpu.SemaphoreType.DMA
    block = (BLOCKS, V, V)
    parts = pl.pallas_call(
        kernel,
        out_shape=(
            pltpu.VMEM(block, bf16), pltpu.VMEM(block, f32), pltpu.VMEM(block, f32),
            pltpu.VMEM((2 * len(LAST), V, V), f32), pltpu.VMEM((8, 128), i32),
        ),
        in_specs=[hbm] * 11,
        out_specs=(vmem,) * 5,
        scratch_shapes=[
            pltpu.SMEM((LINKS, 1, BLOCKS), i32), pltpu.SMEM((BLOCKS, LINKS), i32), pltpu.SMEM((BLOCKS, LINKS), i32),
            pltpu.SMEM((BLOCKS,), i32), pltpu.SMEM((32, 32), f32), pltpu.SMEM((32,), f32), pltpu.VMEM((BLOCKS, V), f32),
            pltpu.VMEM(block, bf16),
            pltpu.VMEM((TASKS, V, V), bf16),
            pltpu.VMEM((TASKS, V, V), bf16),
            pltpu.VMEM((8 * BLOCKS, V, V), bf16),
            pltpu.VMEM((N_COUP * CAP, V, V), bf16),
            pltpu.VMEM((2 * len(LAST), V, V), bf16),
            [pltpu.VMEM((BLOCKS, HALF, V), bf16)] * (2 * len(INNER)),
            pltpu.VMEM((2 * len(LEAVES), CAP, HALF, V), bf16),
            pltpu.VMEM((8, 128), i32),
            pltpu.VMEM((4, 8, 128), i32),
            pltpu.SMEM((8, 128), i32),
            pltpu.SMEM((4, 8, 128), i32),
            dma((7,)), dma((5,)), dma((4,)), dma((4,)), dma((5,)),
            dma((2, len(NODES), 2)), dma((2, len(NODES), 2)), dma((6,)), dma((6,)), dma((8,)), dma((8,)),
        ],
        compiler_params=pltpu.CompilerParams(
            collective_id=0, has_side_effects=True, vmem_limit_bytes=52 * 2**20
        ),
        cost_estimate=pl.CostEstimate(flops=96 * 4 * V**3, bytes_accessed=16 * 2**20, transcendentals=0),
        name="residual_iteration",
    )(
        jnp.transpose(row_peer, (1, 2, 0)), row_offset, column_partner, pno_count, occ_fock, occ_energy, pno_energy,
        amplitudes, integrals,
        row_intersection.reshape(TASKS, V, V), column_intersection.reshape(TASKS, V, V),
    )
    return pl.pallas_call(
        results_kernel,
        out_shape=(jax.ShapeDtypeStruct(block, bf16), jax.ShapeDtypeStruct(block, bf16), pltpu.VMEM(block, f32)),
        input_output_aliases={1: 2},
        in_specs=[vmem] * 5,
        out_specs=(hbm, hbm, vmem),
        scratch_shapes=[pltpu.VMEM(block, bf16), pltpu.VMEM(block, bf16), dma((2, BLOCKS))],
        compiler_params=pltpu.CompilerParams(vmem_limit_bytes=52 * 2**20),
        cost_estimate=pl.CostEstimate(flops=0, bytes_accessed=4 * 2**20, transcendentals=0),
        name="results",
    )(*(pltpu.with_memory_space_constraint(a, pltpu.VMEM) for a in parts))[:2]


def solution(mesh):
    whole = P(("pair", "coup"))
    return jax.shard_map(
        on_device,
        mesh=mesh,
        in_specs=(whole, whole, whole, P(), P(), whole, whole, whole, whole, whole, whole),
        out_specs=(whole, whole),
        check_vma=False,
    )
```

```python
import functools

import jax
import jax.numpy as jnp
from jax import lax
from jax.experimental import pallas as pl
from jax.experimental.pallas import tpu as pltpu
from jax.sharding import PartitionSpec as P

MESH = pl.DeviceIdType.MESH
V = 256
HALF = 128
BLOCKS = 8
LINKS = 6
TASKS = BLOCKS * LINKS
CAP = 4
SIDE = 4
N_COUP = 16

TREE = {
    (0, 1): (0, 0), (3, 0): (0, 0), (1, 1): (0, 1), (3, 3): (3, 0), (1, 2): (1, 1),
    (0, 3): (0, 0), (1, 0): (0, 0), (0, 2): (0, 1), (2, 0): (3, 0), (2, 1): (1, 1), (2, 3): (3, 3),
    (3, 1): (0, 1), (3, 2): (3, 3), (1, 3): (1, 2), (2, 2): (1, 2),
}
ROOT = (0, 0)
ORDER = [
    (0, (0, 1), 0), (1, (0, 1), 0), (0, (3, 0), 0), (1, (3, 0), 0),
    (0, (0, 1), 1), (1, (0, 1), 1), (0, (3, 0), 1), (1, (3, 0), 1),
    (0, (1, 1), 0), (1, (1, 1), 0), (0, (3, 3), 0), (1, (3, 3), 0),
    (0, (1, 1), 1), (1, (1, 1), 1), (0, (3, 3), 1), (1, (3, 3), 1),
    (0, (1, 2), 0), (1, (1, 2), 0), (0, (1, 0), None), (1, (1, 0), None),
    (0, (1, 2), 1), (1, (1, 2), 1), (0, (2, 0), None), (1, (2, 0), None),
    (0, (2, 1), None), (1, (2, 1), None), (0, (0, 3), None), (1, (0, 3), None),
    (0, (2, 3), None), (1, (2, 3), None), (0, (3, 2), None), (1, (3, 2), None),
    (0, (3, 1), None), (1, (3, 1), None), (0, (1, 3), None), (1, (1, 3), None),
    (0, (0, 2), 0), (1, (0, 2), 0), (0, (2, 2), 0), (1, (2, 2), 0),
    (0, (0, 2), 1), (1, (0, 2), 1), (0, (2, 2), 1), (1, (2, 2), 1),
]
LAST = [(0, 2), (2, 2)]
INNER = [n for n in TREE if n in TREE.values()]
LEAVES = [n for n in TREE if n not in TREE.values()]
GROUPS = {}
for _i, _copy in enumerate(ORDER):
    GROUPS.setdefault((_i // 4, _copy[1] in LEAVES), []).append(_copy)
GROUPS = list(GROUPS.values())
DIRS = [(1, 0), (3, 0), (0, 1), (0, 3)]


def sign(tree, node):
    return node if tree == 0 else ((-node[0]) % SIDE, (-node[1]) % SIDE)


def kernel(
    peer_h, offset_h, partner_h, count_h, fock_h, occ_h, energy_h, amp, integ, s_row, s_col,
    own, full_part, inv_den, late_part, late_pair,
    peer, offset, partner, count, fock, occ, energy,
    k_in, srow, scol, cols, slots, late, inner, packed,
    lists, lists_in, lists_s, lists_in_s,
    small_sem, in_sem, list_send, list_recv, list_local, row_send, row_recv, col_send, y_recv, c_recv,
):
    pair, coup = lax.axis_index("pair"), lax.axis_index("coup")
    y, core = pair // 2, pair % 2
    z, x = coup // SIDE, coup % SIDE

    def coup_at(dz, dx):
        return lax.rem(z + dz, SIDE) * SIDE + lax.rem(x + dx, SIDE)

    def pair_at(dy, dc=0):
        return lax.rem(y + dy, SIDE) * 2 + lax.rem(core + dc, 2)

    small = [
        (peer_h, peer), (offset_h, offset), (partner_h, partner), (count_h, count), (fock_h, fock), (occ_h, occ),
        (energy_h, energy),
    ]
    large = [(amp, own), (amp, cols.at[pl.ds(pair * BLOCKS, BLOCKS)]), (integ, k_in), (s_col, scol), (s_row, srow)]
    small_loads = [pltpu.make_async_copy(a, b, small_sem.at[i]) for i, (a, b) in enumerate(small)]
    loads = [pltpu.make_async_copy(a, b, in_sem.at[i]) for i, (a, b) in enumerate(large)]

    barrier = pltpu.get_barrier_semaphore()
    friends = [(pair, coup_at(*d)) for d in DIRS] + [(pair_at(d), coup) for d in (1, 3)] + [(pair_at(0, 1), coup)]
    for friend in friends:
        pl.semaphore_signal(barrier, inc=1, device_id=friend, device_id_type=MESH)
    for load in small_loads:
        load.start()
    pl.semaphore_wait(barrier, len(friends))

    def rows_of(tree):
        return pl.ds(tree * HALF, HALF)

    def leaf_place(source, tree, node, part):
        if part is None:
            return slots.at[pl.ds(source * CAP, CAP), rows_of(tree), :]
        if part == 0:
            return slots.at[pl.ds(source * CAP, 2), rows_of(tree), :]
        return late.at[pl.ds(LAST.index(node) * 2, 2), rows_of(tree), :]

    def row_copy(tree, node, part):
        at, to = sign(tree, TREE[node]), sign(tree, node)
        step = ((to[0] - at[0]) % SIDE, (to[1] - at[1]) % SIDE)
        source = coup_at((-at[0]) % SIDE, (-at[1]) % SIDE)
        if node in INNER:
            four = pl.ds(part * 4, 4)
            src = amp.at[four, rows_of(tree), :] if at == ROOT else inner_of(tree, TREE[node]).at[four]
            dst = inner_of(tree, node).at[four]
        else:
            src = packed.at[tree * len(LEAVES) + LEAVES.index(node)]
            if part is not None:
                src = src.at[pl.ds(part * 2, 2)]
            dst = leaf_place(source, tree, node, part)
        group = [(tree, node, part) in g for g in GROUPS].index(True)
        return pltpu.make_async_remote_copy(
            src_ref=src, dst_ref=dst, send_sem=row_send.at[tree], recv_sem=row_recv.at[group],
            device_id=(pair, coup_at(*step)), device_id_type=MESH,
        )

    def source_at(tree, node):
        n = sign(tree, node)
        return coup_at((-n[0]) % SIDE, (-n[1]) % SIDE)

    def inner_of(tree, node):
        return inner[tree * len(INNER) + INNER.index(node)]

    def take(ref, semaphore):
        pltpu.make_async_copy(ref, ref, semaphore).wait()

    def col_region(source, part):
        return cols.at[pl.ds(source * BLOCKS + part * 4, 4)]

    def y_copy(dy, part, hop):
        source = pair if hop == 0 else pair_at((-dy) % SIDE)
        src = amp.at[pl.ds(part * 4, 4)] if hop == 0 else col_region(source, part)
        i = (0 if dy == 1 else 3) + (part if hop == 0 else 2)
        return pltpu.make_async_remote_copy(
            src_ref=src, dst_ref=col_region(source, part), send_sem=col_send.at[0], recv_sem=y_recv.at[i],
            device_id=(pair_at(dy), coup), device_id_type=MESH,
        )

    def c_copy(dy, part):
        source = pair_at(dy)
        src = amp.at[pl.ds(part * 4, 4)] if dy == 0 else col_region(source, part)
        return pltpu.make_async_remote_copy(
            src_ref=src, dst_ref=col_region(source, part), send_sem=col_send.at[0], recv_sem=c_recv.at[0],
            device_id=(pair_at(0, 1), coup), device_id_type=MESH,
        )

    def start(copy):
        copy.start()

    position = 0
    arrived = set()

    def await_rows(tree, node, part):
        group = [(tree, node, part) in g for g in GROUPS].index(True)
        if group not in arrived:
            arrived.add(group)
            halves = sum(2 if n in LAST else 4 for _, n, _ in GROUPS[group])
            take(packed.at[pl.ds(0, halves // 4)], row_recv.at[group])

    def send_rows(upto):
        nonlocal position
        while position < upto:
            tree, node, part = ORDER[position]
            if TREE[node] != ROOT:
                for half in (0, 1) if node in LEAVES else (part,):
                    await_rows(tree, TREE[node], half)
            if node in LEAVES and part != 1:
                pack(tree, node)
            start(row_copy(tree, node, part))
            position += 1

    def pack(tree, node):
        at, to = sign(tree, TREE[node]), sign(tree, node)
        step = ((to[0] - at[0]) % SIDE, (to[1] - at[1]) % SIDE)
        source = coup_at((-at[0]) % SIDE, (-at[1]) % SIDE)
        d = DIRS.index(step)
        for t in range(CAP):
            which = lists_in_s[d, 0, source * CAP + t]
            packed[tree * len(LEAVES) + LEAVES.index(node), t] = block_of(tree, TREE[node], which)

    def block_of(tree, node, which):
        if node == ROOT:
            return own[which, rows_of(tree), :]
        return inner_of(tree, node)[which]

    def keep(tree, node):
        source = source_at(tree, node)
        for half in range(2):
            await_rows(tree, node, half)
        for t in range(CAP):
            which = lists_s[0, source * CAP + t]
            slots[source * CAP + t, rows_of(tree), :] = block_of(tree, node, which)

    send_rows(8)
    start(y_copy(1, 0, 0))
    start(y_copy(3, 1, 0))
    start(y_copy(1, 1, 0))
    start(y_copy(3, 0, 0))
    start(c_copy(0, 0))
    start(c_copy(0, 1))
    for load in loads:
        load.start()
    for load in small_loads:
        load.wait()

    lane = lax.broadcasted_iota(jnp.int32, (1, 128), 1)

    def peers_step(r, peers):
        return jnp.where(lane == r, peer[r % LINKS, 0, r // LINKS], peers)

    peers = lax.fori_loop(0, TASKS, peers_step, jnp.full((1, 128), -1, jnp.int32), unroll=8)

    def list_step(r, carry):
        wanted, row_of, counts, rank = carry
        p = peer[r % LINKS, 0, r // LINKS]
        local = (r // LINKS // 2) * 2 + offset[r // LINKS, r % LINKS]
        match = (lane // CAP) == p
        hit = match & (lane % CAP == counts)
        return (
            jnp.where(hit, local, wanted),
            jnp.where(hit, r, row_of),
            jnp.where(match, counts + 1, counts),
            rank + jnp.where((lane > r) & (peers == p), 1, 0),
        )

    zero = jnp.zeros((1, 128), jnp.int32)
    wanted, row_of, _, rank = lax.fori_loop(0, TASKS, list_step, (zero, zero - 1, zero, zero), unroll=8)
    lists[0:1, :] = wanted
    lists[1:2, :] = row_of
    lists[2:3, :] = jnp.maximum(peers, 0) * CAP + rank

    def list_copy(i):
        return pltpu.make_async_remote_copy(
            src_ref=lists, dst_ref=lists_in.at[i], send_sem=list_send.at[0], recv_sem=list_recv.at[0],
            device_id=(pair, coup_at((-DIRS[i][0]) % SIDE, (-DIRS[i][1]) % SIDE)), device_id_type=MESH,
        )

    for i in range(4):
        start(list_copy(i))
    to_scalars = pltpu.make_async_copy(lists, lists_s, list_local.at[1])
    to_scalars.start()

    send_rows(12)

    for load in loads[:3]:
        load.wait()

    def first_part(p, _):
        e = energy[pl.ds(p, 1), :]
        across = jnp.broadcast_to(e, (V, V))
        i, j = pair * 4 + p // 2, coup * 2 + p % 2
        den = across + across.T - occ[i] - occ[j]
        cur = own[p].astype(jnp.float32)
        full_part[p] = k_in[p].astype(jnp.float32) + den * cur
        inv_den[p] = 1.0 / den
        return 0

    lax.fori_loop(0, 2, first_part, 0)
    send_rows(16)
    y_copy(1, 0, 0).wait_recv()
    start(y_copy(1, 0, 1))
    start(c_copy(3, 0))
    y_copy(3, 1, 0).wait_recv()
    start(y_copy(3, 1, 1))
    start(c_copy(1, 1))
    to_scalars.wait()
    take(lists_in, list_recv.at[0])
    move = pltpu.make_async_copy(lists_in, lists_in_s, list_local.at[0])
    move.start()
    move.wait()

    lax.fori_loop(2, 8, first_part, 0)
    for n in LAST:
        for t in (2, 3):
            slots[coup_at((-n[0]) % SIDE, (-n[1]) % SIDE) * CAP + t] = jnp.zeros((V, V), jnp.bfloat16)
    for t in range(CAP):
        slots[coup * CAP + t] = own[lists_s[0, coup * CAP + t]]

    def product(a, b, transposed=False):
        dims = (((1,), (1 if transposed else 0,)), ((), ()))
        return lax.dot_general(a, b, dims, preferred_element_type=jnp.float32)

    def link_of(slot, source):
        r = lists_s[1, slot]
        some = jnp.maximum(r, 0)
        f = fock[source * 2 + lists_s[0, slot] % 2, coup * 2 + (some // LINKS) % 2]
        return some, jnp.where(r < 0, 0.0, f)

    def row_first(*nodes):
        for n in nodes:
            source_ready(n)
        for n in nodes:
            source = coup_at((-n[0]) % SIDE, (-n[1]) % SIDE)
            for t in range(2 if n in LAST else CAP):
                slot = source * CAP + t
                r, f = link_of(slot, source)
                slots[slot] = (f * product(srow[r], slots[slot])).astype(jnp.bfloat16)

    def wide(blocks):
        return jnp.concatenate(blocks, axis=1)

    def col_pair(p, _):
        i, parity = pair * 4 + p // 2, p % 2
        parts = []
        for s in range(LINKS):
            q = partner[p, s]
            t = cols[(q // 4) * BLOCKS + (q % 4) * 2 + parity]
            parts.append((fock[i, q] * product(scol[p * LINKS + s], t)).astype(jnp.bfloat16))
        intersections = [scol[p * LINKS + s] for s in range(LINKS)]
        full_part[p] = full_part[p] - product(wide(parts), wide(intersections), True)
        return 0

    def source_ready(n):
        for tree in range(2):
            m = sign(tree, n)
            if m in LEAVES:
                await_rows(tree, m, 0 if m in LAST else None)

    for n in ((0, 1), (3, 0)):
        for tree in range(2):
            keep(tree, n)
    send_rows(20)
    loads[4].wait()
    row_first(ROOT)
    y_copy(1, 1, 0).wait_recv()
    start(c_copy(3, 1))
    y_copy(3, 0, 0).wait_recv()
    start(c_copy(1, 0))
    send_rows(34)
    for n in ((1, 1), (3, 3)):
        for tree in range(2):
            keep(tree, n)
    row_first((1, 1), (3, 3))
    row_first((1, 0), (3, 0))
    loads[3].wait()
    send_rows(44)
    y_copy(1, 0, 1).wait_recv()
    start(c_copy(2, 0))
    y_copy(3, 1, 1).wait_recv()
    start(c_copy(2, 1))
    for tree in range(2):
        keep(tree, (1, 2))
    row_first((2, 0))
    take(cols.at[pl.ds(0, 4 * BLOCKS)], c_recv.at[0])
    lax.fori_loop(0, 3, col_pair, 0)
    row_first((0, 1), (0, 3))
    lax.fori_loop(3, 8, col_pair, 0)
    row_first((2, 1), (2, 3), (1, 2), (3, 2))
    row_first((1, 3), (3, 1))
    row_first((0, 2), (2, 2))

    row_id = lax.broadcasted_iota(jnp.int32, (V, 1), 0)
    col_id = lax.broadcasted_iota(jnp.int32, (1, V), 1)

    def mask_of(p):
        return (row_id < count[p]).astype(jnp.float32) * (col_id < count[p]).astype(jnp.float32)

    for p in range(BLOCKS):
        rows = [p * LINKS + s for s in range(LINKS)]
        mask = mask_of(p)
        term = product(wide([slots[lists_s[2, r]] for r in rows]), wide([srow[r] for r in rows]), True)
        full_part[p] = mask * (full_part[p] - term)
        own[p] = (mask * own[p].astype(jnp.float32)).astype(jnp.bfloat16)

    for tree in range(2):
        for n in LAST:
            await_rows(tree, n, 1)
    middles = []
    for u in range(2 * len(LAST)):
        n = LAST[u // 2]
        source = coup_at((-n[0]) % SIDE, (-n[1]) % SIDE)
        r, f = link_of(source * CAP + 2 + u % 2, source)
        middles.append((r, (f * product(srow[r], late[u])).astype(jnp.bfloat16)))
    for u, (r, middle) in enumerate(middles):
        p = r // LINKS
        late_part[u] = mask_of(p) * product(middle, srow[r], True)
        late_pair[u : u + 1, :] = jnp.full((1, 128), p, jnp.int32)

    take(lists_in, list_send.at[0])
    take(cols.at[pl.ds(0, 7 * BLOCKS)], col_send.at[0])
    for tree in range(2):
        take(packed, row_send.at[tree])


def results_kernel(own, _, inv_den, late_part, late_pair, res_out, new_out, full_part, res_v, new_v, sem):
    stores = []
    pairs = [jnp.max(late_pair[u : u + 1, :]) for u in range(2 * len(LAST))]
    for u, p in enumerate(pairs):
        full_part[p] = full_part[p] - late_part[u]
    for p in range(BLOCKS):
        full = full_part[p]
        res_v[p] = full.astype(jnp.bfloat16)
        new_v[p] = (own[p].astype(jnp.float32) - full * inv_den[p]).astype(jnp.bfloat16)
        stores.append(pltpu.make_async_copy(res_v.at[p], res_out.at[p], sem.at[0, p]))
        stores.append(pltpu.make_async_copy(new_v.at[p], new_out.at[p], sem.at[1, p]))
        stores[-2].start()
        stores[-1].start()
    for store in stores:
        store.wait()


def on_device(
    amplitudes, integrals, pno_energy, occ_energy, occ_fock, row_intersection, column_intersection,
    row_peer, row_offset, column_partner, pno_count,
):
    hbm, vmem = pl.BlockSpec(memory_space=pl.ANY), pl.BlockSpec(memory_space=pltpu.VMEM)
    bf16, f32, i32 = jnp.bfloat16, jnp.float32, jnp.int32
    dma = pltpu.SemaphoreType.DMA
    block = (BLOCKS, V, V)
    parts = pl.pallas_call(
        kernel,
        out_shape=(
            pltpu.VMEM(block, bf16), pltpu.VMEM(block, f32), pltpu.VMEM(block, f32),
            pltpu.VMEM((2 * len(LAST), V, V), f32), pltpu.VMEM((8, 128), i32),
        ),
        in_specs=[hbm] * 11,
        out_specs=(vmem,) * 5,
        scratch_shapes=[
            pltpu.SMEM((LINKS, 1, BLOCKS), i32), pltpu.SMEM((BLOCKS, LINKS), i32), pltpu.SMEM((BLOCKS, LINKS), i32),
            pltpu.SMEM((BLOCKS,), i32), pltpu.SMEM((32, 32), f32), pltpu.SMEM((32,), f32), pltpu.VMEM((BLOCKS, V), f32),
            pltpu.VMEM(block, bf16),
            pltpu.VMEM((TASKS, V, V), bf16),
            pltpu.VMEM((TASKS, V, V), bf16),
            pltpu.VMEM((8 * BLOCKS, V, V), bf16),
            pltpu.VMEM((N_COUP * CAP, V, V), bf16),
            pltpu.VMEM((2 * len(LAST), V, V), bf16),
            [pltpu.VMEM((BLOCKS, HALF, V), bf16)] * (2 * len(INNER)),
            pltpu.VMEM((2 * len(LEAVES), CAP, HALF, V), bf16),
            pltpu.VMEM((8, 128), i32),
            pltpu.VMEM((4, 8, 128), i32),
            pltpu.SMEM((8, 128), i32),
            pltpu.SMEM((4, 8, 128), i32),
            dma((7,)), dma((5,)), dma((1,)), dma((1,)), dma((2,)), dma((2,)), dma((len(GROUPS),)), dma((1,)), dma((6,)),
            dma((1,)),
        ],
        compiler_params=pltpu.CompilerParams(
            collective_id=0, has_side_effects=True, vmem_limit_bytes=52 * 2**20
        ),
        cost_estimate=pl.CostEstimate(flops=96 * 4 * V**3, bytes_accessed=16 * 2**20, transcendentals=0),
        name="residual_iteration",
    )(
        jnp.transpose(row_peer, (1, 2, 0)), row_offset, column_partner, pno_count, occ_fock, occ_energy, pno_energy,
        amplitudes, integrals,
        row_intersection.reshape(TASKS, V, V), column_intersection.reshape(TASKS, V, V),
    )
    return pl.pallas_call(
        results_kernel,
        out_shape=(jax.ShapeDtypeStruct(block, bf16), jax.ShapeDtypeStruct(block, bf16), pltpu.VMEM(block, f32)),
        input_output_aliases={1: 2},
        in_specs=[vmem] * 5,
        out_specs=(hbm, hbm, vmem),
        scratch_shapes=[pltpu.VMEM(block, bf16), pltpu.VMEM(block, bf16), dma((2, BLOCKS))],
        compiler_params=pltpu.CompilerParams(vmem_limit_bytes=52 * 2**20),
        cost_estimate=pl.CostEstimate(flops=0, bytes_accessed=4 * 2**20, transcendentals=0),
        name="results",
    )(*(pltpu.with_memory_space_constraint(a, pltpu.VMEM) for a in parts))[:2]


def solution(mesh):
    whole = P(("pair", "coup"))
    return jax.shard_map(
        on_device,
        mesh=mesh,
        in_specs=(whole, whole, whole, P(), P(), whole, whole, whole, whole, whole, whole),
        out_specs=(whole, whole),
        check_vma=False,
    )
```

```python
import functools

import jax
import jax.numpy as jnp
from jax import lax
from jax.experimental import pallas as pl
from jax.experimental.pallas import tpu as pltpu
from jax.sharding import PartitionSpec as P

MESH = pl.DeviceIdType.MESH
V = 256
HALF = 128
BLOCKS = 8
LINKS = 6
TASKS = BLOCKS * LINKS
CAP = 4
SIDE = 4
N_COUP = 16

TREE = {
    (0, 1): (0, 0), (3, 0): (0, 0), (1, 1): (0, 1), (3, 3): (3, 0), (1, 2): (1, 1),
    (0, 3): (0, 0), (1, 0): (0, 0), (0, 2): (0, 1), (2, 0): (3, 0), (2, 1): (1, 1), (2, 3): (3, 3),
    (3, 1): (0, 1), (3, 2): (3, 3), (1, 3): (1, 2), (2, 2): (1, 2),
}
ROOT = (0, 0)
ORDER = [
    (0, (0, 1), 0), (1, (0, 1), 0), (0, (3, 0), 0), (1, (3, 0), 0),
    (0, (0, 1), 1), (1, (0, 1), 1), (0, (3, 0), 1), (1, (3, 0), 1),
    (0, (1, 1), 0), (1, (1, 1), 0), (0, (3, 3), 0), (1, (3, 3), 0),
    (0, (1, 1), 1), (1, (1, 1), 1), (0, (3, 3), 1), (1, (3, 3), 1),
    (0, (1, 2), 0), (1, (1, 2), 0), (0, (1, 0), None), (1, (1, 0), None),
    (0, (1, 2), 1), (1, (1, 2), 1), (0, (2, 0), None), (1, (2, 0), None),
    (0, (2, 1), None), (1, (2, 1), None), (0, (0, 3), None), (1, (0, 3), None),
    (0, (2, 3), None), (1, (2, 3), None), (0, (3, 2), None), (1, (3, 2), None),
    (0, (3, 1), None), (1, (3, 1), None), (0, (1, 3), None), (1, (1, 3), None),
    (0, (0, 2), 0), (1, (0, 2), 0), (0, (2, 2), 0), (1, (2, 2), 0),
    (0, (0, 2), 1), (1, (0, 2), 1), (0, (2, 2), 1), (1, (2, 2), 1),
]
LAST = [(0, 2), (2, 2)]
INNER = [n for n in TREE if n in TREE.values()]
LEAVES = [n for n in TREE if n not in TREE.values()]
GROUPS = {}
for _i, _copy in enumerate(ORDER):
    GROUPS.setdefault((_i // 4, _copy[1] in LEAVES), []).append(_copy)
GROUPS = list(GROUPS.values())
DIRS = [(1, 0), (3, 0), (0, 1), (0, 3)]


def sign(tree, node):
    return node if tree == 0 else ((-node[0]) % SIDE, (-node[1]) % SIDE)


def kernel(
    peer_h, offset_h, partner_h, count_h, fock_h, occ_h, energy_h, amp, integ, s_row, s_col,
    own, full_part, inv_den, late_part, late_pair,
    peer, offset, partner, count, fock, occ, energy,
    k_in, srow, scol, cols, slots, late, inner, packed,
    lists, lists_in, lists_s, lists_in_s,
    small_sem, in_sem, list_send, list_recv, list_local, row_send, row_recv, col_send, y_recv, c_recv,
):
    pair, coup = lax.axis_index("pair"), lax.axis_index("coup")
    y, core = pair // 2, pair % 2
    z, x = coup // SIDE, coup % SIDE

    def coup_at(dz, dx):
        return lax.rem(z + dz, SIDE) * SIDE + lax.rem(x + dx, SIDE)

    def pair_at(dy, dc=0):
        return lax.rem(y + dy, SIDE) * 2 + lax.rem(core + dc, 2)

    small = [
        (peer_h, peer), (offset_h, offset), (partner_h, partner), (count_h, count), (fock_h, fock), (occ_h, occ),
        (energy_h, energy),
    ]
    large = [(amp, own), (amp, cols.at[pl.ds(pair * BLOCKS, BLOCKS)]), (integ, k_in), (s_col, scol), (s_row, srow)]
    small_loads = [pltpu.make_async_copy(a, b, small_sem.at[i]) for i, (a, b) in enumerate(small)]
    loads = [pltpu.make_async_copy(a, b, in_sem.at[max(i - 2, 0)]) for i, (a, b) in enumerate(large)]

    barrier = pltpu.get_barrier_semaphore()
    friends = [(pair, coup_at(*d)) for d in DIRS] + [(pair_at(d), coup) for d in (1, 3)] + [(pair_at(0, 1), coup)]
    for friend in friends:
        pl.semaphore_signal(barrier, inc=1, device_id=friend, device_id_type=MESH)
    for load in small_loads:
        load.start()
    pl.semaphore_wait(barrier, len(friends))

    def rows_of(tree):
        return pl.ds(tree * HALF, HALF)

    def leaf_place(source, tree, node, part):
        if part is None:
            return slots.at[pl.ds(source * CAP, CAP), rows_of(tree), :]
        if part == 0:
            return slots.at[pl.ds(source * CAP, 2), rows_of(tree), :]
        return late.at[pl.ds(LAST.index(node) * 2, 2), rows_of(tree), :]

    def row_copy(tree, node, part):
        at, to = sign(tree, TREE[node]), sign(tree, node)
        step = ((to[0] - at[0]) % SIDE, (to[1] - at[1]) % SIDE)
        source = coup_at((-at[0]) % SIDE, (-at[1]) % SIDE)
        if node in INNER:
            four = pl.ds(part * 4, 4)
            src = amp.at[four, rows_of(tree), :] if at == ROOT else inner_of(tree, TREE[node]).at[four]
            dst = inner_of(tree, node).at[four]
        else:
            src = packed.at[tree * len(LEAVES) + LEAVES.index(node)]
            if part is not None:
                src = src.at[pl.ds(part * 2, 2)]
            dst = leaf_place(source, tree, node, part)
        group = [(tree, node, part) in g for g in GROUPS].index(True)
        return pltpu.make_async_remote_copy(
            src_ref=src, dst_ref=dst, send_sem=row_send.at[tree], recv_sem=row_recv.at[group],
            device_id=(pair, coup_at(*step)), device_id_type=MESH,
        )

    def source_at(tree, node):
        n = sign(tree, node)
        return coup_at((-n[0]) % SIDE, (-n[1]) % SIDE)

    def inner_of(tree, node):
        return inner[tree * len(INNER) + INNER.index(node)]

    def take(ref, semaphore):
        pltpu.make_async_copy(ref, ref, semaphore).wait()

    def col_region(source, part):
        return cols.at[pl.ds(source * BLOCKS + part * 4, 4)]

    def y_copy(dy, part, hop):
        source = pair if hop == 0 else pair_at((-dy) % SIDE)
        src = amp.at[pl.ds(part * 4, 4)] if hop == 0 else col_region(source, part)
        i = (0 if dy == 1 else 3) + (part if hop == 0 else 2)
        return pltpu.make_async_remote_copy(
            src_ref=src, dst_ref=col_region(source, part), send_sem=col_send.at[0], recv_sem=y_recv.at[i],
            device_id=(pair_at(dy), coup), device_id_type=MESH,
        )

    def c_copy(dy, part):
        source = pair_at(dy)
        src = amp.at[pl.ds(part * 4, 4)] if dy == 0 else col_region(source, part)
        return pltpu.make_async_remote_copy(
            src_ref=src, dst_ref=col_region(source, part), send_sem=col_send.at[0], recv_sem=c_recv.at[0],
            device_id=(pair_at(0, 1), coup), device_id_type=MESH,
        )

    def start(copy):
        copy.start()

    position = 0
    arrived = set()

    def await_rows(tree, node, part):
        group = [(tree, node, part) in g for g in GROUPS].index(True)
        if group not in arrived:
            arrived.add(group)
            halves = sum(2 if n in LAST else 4 for _, n, _ in GROUPS[group])
            take(packed.at[pl.ds(0, halves // 4)], row_recv.at[group])

    def send_rows(upto):
        nonlocal position
        while position < upto:
            tree, node, part = ORDER[position]
            if TREE[node] != ROOT:
                for half in (0, 1) if node in LEAVES else (part,):
                    await_rows(tree, TREE[node], half)
            if node in LEAVES and part != 1:
                pack(tree, node)
            start(row_copy(tree, node, part))
            position += 1

    def pack(tree, node):
        at, to = sign(tree, TREE[node]), sign(tree, node)
        step = ((to[0] - at[0]) % SIDE, (to[1] - at[1]) % SIDE)
        source = coup_at((-at[0]) % SIDE, (-at[1]) % SIDE)
        d = DIRS.index(step)
        for t in range(CAP):
            which = lists_in_s[d, 0, source * CAP + t]
            packed[tree * len(LEAVES) + LEAVES.index(node), t] = block_of(tree, TREE[node], which)

    def block_of(tree, node, which):
        if node == ROOT:
            return own[which, rows_of(tree), :]
        return inner_of(tree, node)[which]

    def keep(tree, node):
        source = source_at(tree, node)
        for half in range(2):
            await_rows(tree, node, half)
        for t in range(CAP):
            which = lists_s[0, source * CAP + t]
            slots[source * CAP + t, rows_of(tree), :] = block_of(tree, node, which)

    send_rows(8)
    start(y_copy(1, 0, 0))
    start(y_copy(3, 1, 0))
    start(y_copy(1, 1, 0))
    start(y_copy(3, 0, 0))
    start(c_copy(0, 0))
    start(c_copy(0, 1))
    for load in loads:
        load.start()
    for load in small_loads:
        load.wait()

    lane = lax.broadcasted_iota(jnp.int32, (1, 128), 1)

    def peers_step(r, peers):
        return jnp.where(lane == r, peer[r % LINKS, 0, r // LINKS], peers)

    peers = lax.fori_loop(0, TASKS, peers_step, jnp.full((1, 128), -1, jnp.int32), unroll=8)

    def list_step(r, carry):
        wanted, row_of, counts, rank = carry
        p = peer[r % LINKS, 0, r // LINKS]
        local = (r // LINKS // 2) * 2 + offset[r // LINKS, r % LINKS]
        match = (lane // CAP) == p
        hit = match & (lane % CAP == counts)
        return (
            jnp.where(hit, local, wanted),
            jnp.where(hit, r, row_of),
            jnp.where(match, counts + 1, counts),
            rank + jnp.where((lane > r) & (peers == p), 1, 0),
        )

    zero = jnp.zeros((1, 128), jnp.int32)
    wanted, row_of, _, rank = lax.fori_loop(0, TASKS, list_step, (zero, zero - 1, zero, zero), unroll=8)
    lists[0:1, :] = wanted
    lists[1:2, :] = row_of
    lists[2:3, :] = jnp.maximum(peers, 0) * CAP + rank

    def list_copy(i):
        return pltpu.make_async_remote_copy(
            src_ref=lists, dst_ref=lists_in.at[i], send_sem=list_send.at[0], recv_sem=list_recv.at[0],
            device_id=(pair, coup_at((-DIRS[i][0]) % SIDE, (-DIRS[i][1]) % SIDE)), device_id_type=MESH,
        )

    for i in range(4):
        start(list_copy(i))
    to_scalars = pltpu.make_async_copy(lists, lists_s, list_local.at[1])
    to_scalars.start()

    send_rows(12)

    take(cols.at[pl.ds(0, 3 * BLOCKS)], in_sem.at[0])

    def first_part(p, _):
        e = energy[pl.ds(p, 1), :]
        across = jnp.broadcast_to(e, (V, V))
        i, j = pair * 4 + p // 2, coup * 2 + p % 2
        den = across + across.T - occ[i] - occ[j]
        cur = own[p].astype(jnp.float32)
        full_part[p] = k_in[p].astype(jnp.float32) + den * cur
        inv_den[p] = 1.0 / den
        return 0

    lax.fori_loop(0, 2, first_part, 0)
    send_rows(16)
    y_copy(1, 0, 0).wait_recv()
    start(y_copy(1, 0, 1))
    start(c_copy(3, 0))
    y_copy(3, 1, 0).wait_recv()
    start(y_copy(3, 1, 1))
    start(c_copy(1, 1))
    to_scalars.wait()
    take(lists_in, list_recv.at[0])
    move = pltpu.make_async_copy(lists_in, lists_in_s, list_local.at[0])
    move.start()
    move.wait()

    lax.fori_loop(2, 8, first_part, 0)
    for n in LAST:
        for t in (2, 3):
            slots[coup_at((-n[0]) % SIDE, (-n[1]) % SIDE) * CAP + t] = jnp.zeros((V, V), jnp.bfloat16)
    for t in range(CAP):
        slots[coup * CAP + t] = own[lists_s[0, coup * CAP + t]]

    def product(a, b, transposed=False):
        dims = (((1,), (1 if transposed else 0,)), ((), ()))
        return lax.dot_general(a, b, dims, preferred_element_type=jnp.float32)

    def link_of(slot, source):
        r = lists_s[1, slot]
        some = jnp.maximum(r, 0)
        f = fock[source * 2 + lists_s[0, slot] % 2, coup * 2 + (some // LINKS) % 2]
        return some, jnp.where(r < 0, 0.0, f)

    def row_first(*nodes):
        for n in nodes:
            source_ready(n)
        for n in nodes:
            source = coup_at((-n[0]) % SIDE, (-n[1]) % SIDE)
            for t in range(2 if n in LAST else CAP):
                slot = source * CAP + t
                r, f = link_of(slot, source)
                slots[slot] = (f * product(srow[r], slots[slot])).astype(jnp.bfloat16)

    def wide(blocks):
        return jnp.concatenate(blocks, axis=1)

    def col_pair(p, _):
        i, parity = pair * 4 + p // 2, p % 2
        parts = []
        for s in range(LINKS):
            q = partner[p, s]
            t = cols[(q // 4) * BLOCKS + (q % 4) * 2 + parity]
            parts.append((fock[i, q] * product(scol[p * LINKS + s], t)).astype(jnp.bfloat16))
        intersections = [scol[p * LINKS + s] for s in range(LINKS)]
        full_part[p] = full_part[p] - product(wide(parts), wide(intersections), True)
        return 0

    def source_ready(n):
        for tree in range(2):
            m = sign(tree, n)
            if m in LEAVES:
                await_rows(tree, m, 0 if m in LAST else None)

    for n in ((0, 1), (3, 0)):
        for tree in range(2):
            keep(tree, n)
    send_rows(20)
    loads[4].wait()
    row_first(ROOT)
    y_copy(1, 1, 0).wait_recv()
    start(c_copy(3, 1))
    y_copy(3, 0, 0).wait_recv()
    start(c_copy(1, 0))
    send_rows(34)
    for n in ((1, 1), (3, 3)):
        for tree in range(2):
            keep(tree, n)
    row_first((1, 1), (3, 3))
    row_first((1, 0), (3, 0))
    loads[3].wait()
    send_rows(44)
    y_copy(1, 0, 1).wait_recv()
    start(c_copy(2, 0))
    y_copy(3, 1, 1).wait_recv()
    start(c_copy(2, 1))
    for tree in range(2):
        keep(tree, (1, 2))
    row_first((2, 0))
    take(cols.at[pl.ds(0, 4 * BLOCKS)], c_recv.at[0])
    lax.fori_loop(0, 3, col_pair, 0)
    row_first((0, 1), (0, 3))
    lax.fori_loop(3, 8, col_pair, 0)
    row_first((2, 1), (2, 3), (1, 2), (3, 2))
    row_first((1, 3), (3, 1))
    row_first((0, 2), (2, 2))

    row_id = lax.broadcasted_iota(jnp.int32, (V, 1), 0)
    col_id = lax.broadcasted_iota(jnp.int32, (1, V), 1)

    def mask_of(p):
        return (row_id < count[p]).astype(jnp.float32) * (col_id < count[p]).astype(jnp.float32)

    for p in range(BLOCKS):
        rows = [p * LINKS + s for s in range(LINKS)]
        mask = mask_of(p)
        term = product(wide([slots[lists_s[2, r]] for r in rows]), wide([srow[r] for r in rows]), True)
        full_part[p] = mask * (full_part[p] - term)
        own[p] = (mask * own[p].astype(jnp.float32)).astype(jnp.bfloat16)

    for tree in range(2):
        for n in LAST:
            await_rows(tree, n, 1)
    middles = []
    for u in range(2 * len(LAST)):
        n = LAST[u // 2]
        source = coup_at((-n[0]) % SIDE, (-n[1]) % SIDE)
        r, f = link_of(source * CAP + 2 + u % 2, source)
        middles.append((r, (f * product(srow[r], late[u])).astype(jnp.bfloat16)))
    for u, (r, middle) in enumerate(middles):
        p = r // LINKS
        late_part[u] = mask_of(p) * product(middle, srow[r], True)
        late_pair[u : u + 1, :] = jnp.full((1, 128), p, jnp.int32)

    take(lists_in, list_send.at[0])
    take(cols.at[pl.ds(0, 7 * BLOCKS)], col_send.at[0])
    for tree in range(2):
        take(packed, row_send.at[tree])


def results_kernel(own, _, inv_den, late_part, late_pair, res_out, new_out, full_part, res_v, new_v, sem):
    pairs = [jnp.max(late_pair[u : u + 1, :]) for u in range(2 * len(LAST))]
    for u, p in enumerate(pairs):
        full_part[p] = full_part[p] - late_part[u]
    for p in range(BLOCKS):
        full = full_part[p]
        res_v[p] = full.astype(jnp.bfloat16)
        new_v[p] = (own[p].astype(jnp.float32) - full * inv_den[p]).astype(jnp.bfloat16)
        if p % 2 == 1:
            two = pl.ds(p - 1, 2)
            pltpu.make_async_copy(res_v.at[two], res_out.at[two], sem.at[0]).start()
            pltpu.make_async_copy(new_v.at[two], new_out.at[two], sem.at[1]).start()
    pltpu.make_async_copy(res_v, res_out, sem.at[0]).wait()
    pltpu.make_async_copy(new_v, new_out, sem.at[1]).wait()


def on_device(
    amplitudes, integrals, pno_energy, occ_energy, occ_fock, row_intersection, column_intersection,
    row_peer, row_offset, column_partner, pno_count,
):
    hbm, vmem = pl.BlockSpec(memory_space=pl.ANY), pl.BlockSpec(memory_space=pltpu.VMEM)
    bf16, f32, i32 = jnp.bfloat16, jnp.float32, jnp.int32
    dma = pltpu.SemaphoreType.DMA
    block = (BLOCKS, V, V)
    parts = pl.pallas_call(
        kernel,
        out_shape=(
            pltpu.VMEM(block, bf16), pltpu.VMEM(block, f32), pltpu.VMEM(block, f32),
            pltpu.VMEM((2 * len(LAST), V, V), f32), pltpu.VMEM((8, 128), i32),
        ),
        in_specs=[hbm] * 11,
        out_specs=(vmem,) * 5,
        scratch_shapes=[
            pltpu.SMEM((LINKS, 1, BLOCKS), i32), pltpu.SMEM((BLOCKS, LINKS), i32), pltpu.SMEM((BLOCKS, LINKS), i32),
            pltpu.SMEM((BLOCKS,), i32), pltpu.SMEM((32, 32), f32), pltpu.SMEM((32,), f32), pltpu.VMEM((BLOCKS, V), f32),
            pltpu.VMEM(block, bf16),
            pltpu.VMEM((TASKS, V, V), bf16),
            pltpu.VMEM((TASKS, V, V), bf16),
            pltpu.VMEM((8 * BLOCKS, V, V), bf16),
            pltpu.VMEM((N_COUP * CAP, V, V), bf16),
            pltpu.VMEM((2 * len(LAST), V, V), bf16),
            [pltpu.VMEM((BLOCKS, HALF, V), bf16)] * (2 * len(INNER)),
            pltpu.VMEM((2 * len(LEAVES), CAP, HALF, V), bf16),
            pltpu.VMEM((8, 128), i32),
            pltpu.VMEM((4, 8, 128), i32),
            pltpu.SMEM((8, 128), i32),
            pltpu.SMEM((4, 8, 128), i32),
            dma((7,)), dma((3,)), dma((1,)), dma((1,)), dma((2,)), dma((2,)), dma((len(GROUPS),)), dma((1,)), dma((6,)),
            dma((1,)),
        ],
        compiler_params=pltpu.CompilerParams(
            collective_id=0, has_side_effects=True, vmem_limit_bytes=52 * 2**20
        ),
        cost_estimate=pl.CostEstimate(flops=96 * 4 * V**3, bytes_accessed=16 * 2**20, transcendentals=0),
        name="residual_iteration",
    )(
        jnp.transpose(row_peer, (1, 2, 0)), row_offset, column_partner, pno_count, occ_fock, occ_energy, pno_energy,
        amplitudes, integrals,
        row_intersection.reshape(TASKS, V, V), column_intersection.reshape(TASKS, V, V),
    )
    return pl.pallas_call(
        results_kernel,
        out_shape=(jax.ShapeDtypeStruct(block, bf16), jax.ShapeDtypeStruct(block, bf16), pltpu.VMEM(block, f32)),
        input_output_aliases={1: 2},
        in_specs=[vmem] * 5,
        out_specs=(hbm, hbm, vmem),
        scratch_shapes=[pltpu.VMEM(block, bf16), pltpu.VMEM(block, bf16), dma((2,))],
        compiler_params=pltpu.CompilerParams(vmem_limit_bytes=52 * 2**20),
        cost_estimate=pl.CostEstimate(flops=0, bytes_accessed=4 * 2**20, transcendentals=0),
        name="results",
    )(*(pltpu.with_memory_space_constraint(a, pltpu.VMEM) for a in parts))[:2]


def solution(mesh):
    whole = P(("pair", "coup"))
    return jax.shard_map(
        on_device,
        mesh=mesh,
        in_specs=(whole, whole, whole, P(), P(), whole, whole, whole, whole, whole, whole),
        out_specs=(whole, whole),
        check_vma=False,
    )
```
